32 devices in a mesh: passage: 4 (over z), span: 8 (over y, x, core).
Axes of the slice: x: 2, y: 2, z: 4, core: 2. Of those that a mesh axis runs over, the one named last changes fastest.
Arguments:
- psi_rotor: float32 [6, 64, 64, 128], P(None, 'passage', 'span'), may hold values from -11 to 11
- psi_stator: float32 [6, 64, 64, 128], P(None, 'passage', 'span'), may hold values from -6 to 6
- rhs_rotor: float32 [6, 64, 64, 128], P(None, 'passage', 'span'), may hold values from -6 to 6
- rhs_stator: float32 [6, 64, 64, 128], P(None, 'passage', 'span'), may hold values from -6 to 6
- kappa_rotor: float32 [64, 64, 128], P('passage', 'span'), may hold values from 1 to 4
- kappa_stator: float32 [64, 64, 128], P('passage', 'span'), may hold values from 1 to 4
- rotor_blocks: float32 [7, 6, 6], replicated, may hold values from -0.5 to 1
- stator_blocks: float32 [7, 6, 6], replicated, may hold values from -0.5 to 1
- interface_block: float32 [6, 6], replicated, may hold values from -0.5 to 0.7
- pass_counts: int32 [4], P('passage'), may hold values from 8 to 16
- tile_source: int32 [8], replicated, may hold values from 0 to 7, as said below
Outputs:
- rotor_out: float32 [6, 64, 64, 128], P(None, 'passage', 'span')
- stator_out: float32 [6, 64, 64, 128], P(None, 'passage', 'span')
The draws below stay inside these ranges and needn't reach their ends.
Inputs may be any that keep to these rules, and one draw needn't show every extreme that they name: `tile_source`: each stator span tile names one rotor span tile.
All inputs are finite; a program needn't handle non-finite values.
Results may differ from the reference program's by a relative error of at most 0.00011.
Values sent between devices are 32-bit elements; how exact they have to be, the bound alone decides.
A program may use at most 64 MiB of HBM per device.

```python
import math
import jax
import jax.numpy as jnp
from jax import lax

F = 6
CP = 16
CS = 8
CA = 128
ITERS = 3
PITCH = 64
SPANS = 64
NBLOCKS = 4
NTILES = 8


def draw_psi_rotor(key, part):
    first, second = jax.random.split(key)
    base = jnp.clip(jax.random.normal(first, (F, 1, SPANS, CA), jnp.float32), -4.0, 4.0)
    position = (jnp.arange(PITCH) % CP).astype(jnp.float32) / CP
    wake = (0.4 + 1.6 * position).reshape(1, PITCH, 1, 1)
    noise = 0.7 * jnp.clip(jax.random.normal(second, (F, PITCH, SPANS, CA), jnp.float32), -3.0, 3.0)
    return base * wake + noise


def make_blocks(key):
    eye = jnp.eye(F, dtype=jnp.float32)
    center_noise = jnp.clip(jax.random.normal(jax.random.fold_in(key, 11), (F, F), jnp.float32), -3.0, 3.0)
    center = eye + 0.12 * center_noise * (1.0 - eye)
    side_noise = jnp.clip(jax.random.normal(jax.random.fold_in(key, 12), (6, F, F), jnp.float32), -3.0, 3.0)
    sides = 0.08 * eye[None] + 0.05 * side_noise
    return jnp.concatenate([center[None], sides], axis=0)


def draw_rotor_blocks(key, part):
    return make_blocks(jax.random.fold_in(key, 21))


def draw_stator_blocks(key, part):
    return make_blocks(jax.random.fold_in(key, 22))


def draw_interface_block(key, part):
    eye = jnp.eye(F, dtype=jnp.float32)
    noise = jnp.clip(jax.random.normal(jax.random.fold_in(key, 31), (F, F), jnp.float32), -3.0, 3.0)
    return 0.6 * eye + 0.15 * noise * (1.0 - eye)


def draw_pass_counts(key, part):
    lowest = max(1, CP // 2)
    counts = jax.random.randint(jax.random.fold_in(key, 41), (NBLOCKS,), lowest, CP + 1)
    where = jax.random.randint(jax.random.fold_in(key, 42), (), 0, NBLOCKS)
    counts = counts.at[where].set(CP)
    counts = counts.at[(where + 1) % NBLOCKS].set(lowest)
    return counts.astype(jnp.int32)


def draw_tile_source(key, part):
    source = jax.random.randint(jax.random.fold_in(key, 51), (NTILES,), 0, NTILES)
    where = jax.random.randint(jax.random.fold_in(key, 52), (), 0, NTILES)
    source = source.at[where].set((where + NTILES // 2) % NTILES)
    source = source.at[(where + 1) % NTILES].set(0)
    source = source.at[(where + 2) % NTILES].set(NTILES - 1)
    return source.astype(jnp.int32)


def block_levels(rng, extent, cuts, least, top_value):
    level, own = 1.0, jax.random.fold_in(rng, 6)
    for dim, blocks in cuts:
        heights = jnp.exp(jax.random.uniform(jax.random.fold_in(own, dim), (blocks,), jnp.float32, least / len(cuts), top_value / len(cuts)))
        level = level * jnp.repeat(heights, extent[dim] // blocks).reshape([-1 if axis == dim else 1 for axis in range(len(extent))])
    return level


def normal_values(stream_key, extent, deviation, most, pieces=(), kind=jnp.bfloat16):
    loudness = block_levels(stream_key, extent, pieces, -0.22, 0.18) if pieces else 1.0
    entries = jax.random.normal(stream_key, extent, jnp.float32) * deviation * loudness
    return jnp.minimum(jnp.maximum(entries, -most), most).astype(kind)


def setup_inputs(seed: int = 0) -> dict:
    splits = jax.random.split(jax.random.key(seed), 12)
    return {
        "psi_rotor": draw_psi_rotor(jax.random.fold_in(splits[11], 71), 0),
        "psi_stator": normal_values(splits[1], (F, PITCH, SPANS, CA), 1.0, 6.0, ((1, 4), (2, 8)), jnp.float32),
        "rhs_rotor": normal_values(splits[2], (F, PITCH, SPANS, CA), 1.0, 6.0, ((1, 4), (2, 8)), jnp.float32),
        "rhs_stator": normal_values(splits[3], (F, PITCH, SPANS, CA), 1.0, 6.0, ((1, 4), (2, 8)), jnp.float32),
        "kappa_rotor": jnp.clip(jnp.exp(math.log(4.0) - 1.3862944 * jax.random.uniform(splits[4], (PITCH, SPANS, CA), jnp.float32) ** block_levels(splits[4], (PITCH, SPANS, CA), ((0, 4), (1, 8)), -0.2, 0.2)), 1.0, 4.0),
        "kappa_stator": jnp.clip(jnp.exp(math.log(4.0) - 1.3862944 * jax.random.uniform(splits[5], (PITCH, SPANS, CA), jnp.float32) ** block_levels(splits[5], (PITCH, SPANS, CA), ((0, 4), (1, 8)), -0.2, 0.2)), 1.0, 4.0),
        "rotor_blocks": draw_rotor_blocks(jax.random.fold_in(splits[11], 71), 0),
        "stator_blocks": draw_stator_blocks(jax.random.fold_in(splits[11], 71), 0),
        "interface_block": draw_interface_block(jax.random.fold_in(splits[11], 71), 0),
        "pass_counts": draw_pass_counts(jax.random.fold_in(splits[11], 71), 0),
        "tile_source": draw_tile_source(jax.random.fold_in(splits[11], 71), 0),
    }


def apply_block(block, field):
    return jnp.einsum("fg,gpsa->fpsa", block, field, precision=lax.Precision.HIGHEST)


def operator(field, kappa, blocks):
    pad_span = jnp.pad(field, ((0, 0), (0, 0), (1, 1), (0, 0)))
    pad_axial = jnp.pad(field, ((0, 0), (0, 0), (0, 0), (1, 1)))
    total = apply_block(blocks[1], jnp.roll(field, 1, axis=1))
    total = total + apply_block(blocks[2], jnp.roll(field, -1, axis=1))
    total = total + apply_block(blocks[3], pad_span[:, :, :-2])
    total = total + apply_block(blocks[4], pad_span[:, :, 2:])
    total = total + apply_block(blocks[5], pad_axial[:, :, :, :-2])
    total = total + apply_block(blocks[6], pad_axial[:, :, :, 2:])
    return kappa[None] * apply_block(blocks[0], field) - total


def reference(psi_rotor, psi_stator, rhs_rotor, rhs_stator, kappa_rotor, kappa_stator, rotor_blocks, stator_blocks, interface_block, pass_counts, tile_source):
    pitch_index = jnp.arange(PITCH, dtype=jnp.int32)
    mask = (pitch_index % CP < pass_counts[pitch_index // CP]).astype(jnp.float32)
    for step in range(ITERS):
        face = psi_rotor[:, :, :, CA - 1] * mask[None, :, None]
        face_mean = jnp.sum(face, axis=1) / jnp.sum(mask)
        inflow = face_mean.reshape(F, NTILES, CS)[:, tile_source].reshape(F, SPANS)
        inlet = jnp.dot(interface_block, inflow, precision=lax.Precision.HIGHEST)
        res_rotor = rhs_rotor - operator(psi_rotor, kappa_rotor, rotor_blocks)
        res_stator = rhs_stator - operator(psi_stator, kappa_stator, stator_blocks)
        res_stator = res_stator.at[:, :, :, 0].add(inlet[:, None, :])
        psi_rotor = psi_rotor + 0.8 * res_rotor / kappa_rotor[None]
        psi_stator = psi_stator + 0.8 * res_stator / kappa_stator[None]
    return psi_rotor, psi_stator
```

```python
import functools

import jax
import jax.numpy as jnp
from jax import lax
from jax.experimental import pallas as pl
from jax.experimental.pallas import tpu as pltpu
from jax.sharding import PartitionSpec as P

ITERS = 3
RELAX = 0.8
MESH = pl.DeviceIdType.MESH
F32 = jnp.float32
BF16 = jnp.bfloat16
ROTOR, STATOR = 0, 1
SLOT = 16


def split(x):
    hi = x.astype(BF16)
    lo = (x - hi.astype(F32)).astype(BF16)
    return hi, lo


def kernel(fields, cp, cs, ca, npass, nspan, *refs):
    it = iter(refs)

    def take(n):
        return [next(it) for _ in range(n)]

    psi_in = take(2)
    rhs_in = take(2)
    kap_in = take(2)
    small_in = take(4)
    (counts,) = take(1)
    outs = take(2)
    psi = [take(ITERS) + [outs[r]] for r in range(2)]
    rhs = take(2)
    coef = take(2)
    cen = [take(2) for _ in range(2)]
    ext = [take(2) for _ in range(2)]
    mat = take(2)
    small = take(4)
    blocks, (iface, source) = small[:2], small[2:]
    (precv, ssend, srecv, fsend) = take(4)
    frecv = take(ITERS)
    (in_sem, hs_sem, hr_sem, fs_sem, fr_sem) = take(5)

    nb = fields * cs
    kx = 2 * nb + 16
    plane = cp * cs
    others = npass * nspan - 1

    ip = lax.axis_index("passage")
    js = lax.axis_index("span")
    right = lax.rem(ip + 1, npass)
    left = lax.rem(ip + npass - 1, npass)
    has_next, has_prev = js < nspan - 1, js > 0

    def peer(o):
        return lax.rem(ip + o // nspan, npass), lax.rem(js + o % nspan, nspan)

    def each_peer(body):
        unroll = others if others < 64 else 1
        pl.loop(1, others + 1, unroll=unroll)(body)

    barrier = pltpu.get_barrier_semaphore()
    each_peer(
        lambda o: pl.semaphore_signal(barrier, inc=1, device_id=peer(o), device_id_type=MESH)
    )

    pairs = [
        (psi_in[0], psi[0][0]),
        (psi_in[1], psi[1][0]),
        *zip(small_in, small),
        (kap_in[0], coef[0]),
        (kap_in[1], coef[1]),
        (rhs_in[0], rhs[0]),
        (rhs_in[1], rhs[1]),
    ]
    loads = [pltpu.make_async_copy(a, b, in_sem.at[n]) for n, (a, b) in enumerate(pairs)]
    for c in loads:
        c.start()

    for d, met in ((0, has_prev), (1, has_next)):

        @pl.when(jnp.logical_not(met))
        def _(d=d):
            for r in range(2):
                for k in range(ITERS):
                    srecv[r, k, d] = jnp.zeros((fields, cp, ca), F32)

    def halo_copies(r, k):
        made = []
        for d, p, target in ((0, cp - 1, (right, js)), (1, 0, (left, js))):
            made.append(
                pltpu.make_async_remote_copy(
                    src_ref=psi[r][k].at[:, pl.ds(p * cs, cs), :],
                    dst_ref=precv.at[r, k, d],
                    send_sem=hs_sem.at[r, k, d],
                    recv_sem=hr_sem.at[r, k, d],
                    device_id=target,
                    device_id_type=MESH,
                )
            )
        for d, target in (
            (0, (ip, lax.rem(js + 1, nspan))),
            (1, (ip, lax.rem(js + nspan - 1, nspan))),
        ):
            made.append(
                pltpu.make_async_remote_copy(
                    src_ref=ssend.at[r, k, d],
                    dst_ref=srecv.at[r, k, d],
                    send_sem=hs_sem.at[r, k, 2 + d],
                    recv_sem=hr_sem.at[r, k, 2 + d],
                    device_id=target,
                    device_id_type=MESH,
                )
            )
        return made

    halos = {(r, k): halo_copies(r, k) for r in range(2) for k in range(ITERS)}

    def edge(s):
        return pl.ds(s, cp, stride=cs)

    def pack_span(r, k):
        for d, s in ((0, cs - 1), (1, 0)):
            for f in range(fields):
                ssend[r, k, d, f] = psi[r][k][f, edge(s), :]

    def start_halos(r, k):
        to_right, to_left, to_next, to_prev = halos[r, k]
        to_right.start()
        to_left.start()

        @pl.when(has_next)
        def _():
            to_next.start()

        @pl.when(has_prev)
        def _():
            to_prev.start()

    def finish_sends(r, k):
        to_right, to_left, to_next, to_prev = halos[r, k]
        to_right.wait_send()
        to_left.wait_send()

        @pl.when(has_next)
        def _():
            to_next.wait_send()

        @pl.when(has_prev)
        def _():
            to_prev.wait_send()

    def receive_halos(r, k):
        to_right, to_left, to_next, to_prev = halos[r, k]

        @pl.when(has_prev)
        def _():
            to_next.wait_recv()

        @pl.when(has_next)
        def _():
            to_prev.wait_recv()

        to_right.wait_recv()
        to_left.wait_recv()

    def mix(block, f, parts):
        acc = block(f, 0) * parts[0]
        for g in range(1, fields):
            acc = acc + block(f, g) * parts[g]
        return acc

    def add_halos(r, k):
        new = psi[r][k + 1]
        for d, p in ((0, 0), (1, cp - 1)):
            rows = pl.ds(p * cs, cs)
            c = coef[r][rows, :]
            parts = [precv[r, k, d, g] for g in range(fields)]
            for f in range(fields):
                acc = mix(lambda a, b: blocks[r][a, 1 + d, b], f, parts)
                new[f, rows, :] = new[f, rows, :] + c * acc
        for d, s in ((0, 0), (1, cs - 1)):
            c = coef[r][edge(s), :]
            parts = [srecv[r, k, d, g] for g in range(fields)]
            for f in range(fields):
                acc = mix(lambda a, b: blocks[r][a, 3 + d, b], f, parts)
                new[f, edge(s), :] = new[f, edge(s), :] + c * acc

    lane = lax.broadcasted_iota(jnp.int32, (cs, ca), 1)
    at_slot = lane - SLOT * lax.broadcasted_iota(jnp.int32, (cs, ca), 0)
    wide = lax.broadcasted_iota(jnp.int32, (nb, ca), 1)

    def face_copy(k, o):
        return pltpu.make_async_remote_copy(
            src_ref=fsend.at[k],
            dst_ref=frecv[k].at[o],
            send_sem=fs_sem.at[k],
            recv_sem=fr_sem.at[k],
            device_id=peer(o),
            device_id_type=MESH,
        )

    def pick(x):
        return jnp.sum(x, axis=1, keepdims=True)

    def pack_face(k):
        state = psi[ROTOR][k]
        count = counts[0]
        weights = [jnp.where(p < count, 1.0, 0.0).astype(F32) for p in range(cp)]
        sums = []
        for f in range(fields):
            acc = weights[0] * state[f, pl.ds(0, cs), :]
            for p in range(1, cp):
                acc = acc + weights[p] * state[f, pl.ds(p * cs, cs), :]
            sums.append(jnp.where(lane == ca - 1, acc, 0.0))
        tile = jnp.where(at_slot == fields, jnp.clip(count, 0, cp).astype(F32), 0.0)
        for f in range(fields):
            mixed = mix(lambda a, b: iface[a, b], f, sums)
            tile = jnp.where(at_slot == f, pick(mixed), tile)
        row = jnp.sum(tile, axis=0, keepdims=True)
        fsend[k] = row
        frecv[k][0] = row

    def start_face(k):
        each_peer(lambda o: face_copy(k, o).start())

    def all_faces(k):
        return pltpu.make_async_copy(
            frecv[k].at[pl.ds(1, others)], frecv[k].at[pl.ds(1, others)], fr_sem.at[k]
        )

    def sent_faces(k):
        return pltpu.make_async_copy(
            frecv[k].at[pl.ds(1, others)], frecv[k].at[pl.ds(1, others)], fs_sem.at[k]
        )

    def add_inlet(k):
        all_faces(k).wait()
        away = lax.rem(js - source[js] + nspan, nspan)
        total = frecv[k][away]
        for o in range(1, npass):
            total = total + frecv[k][o * nspan + away]
        total = jnp.broadcast_to(total, (cs, ca))
        count = pick(jnp.where(at_slot == fields, total, 0.0))
        for f in range(fields):
            value = pick(jnp.where(at_slot == f, total, 0.0)) / count
            value = jnp.where(lane == 0, value, 0.0)
            new = psi[STATOR][k + 1]
            for p in range(cp):
                rows = pl.ds(p * cs, cs)
                new[f, rows, :] = new[f, rows, :] + coef[STATOR][rows, :] * value

    def build_matrix(r):
        kk = 5 * nb + 16
        col = lax.broadcasted_iota(jnp.int32, (cs, kk), 1)
        row = lax.broadcasted_iota(jnp.int32, (cs, kk), 0)
        part = col // nb
        g_in = (col - part * nb) // cs
        s_in = col - part * nb - g_in * cs
        which = jnp.full((cs, kk), -1, jnp.int32)
        same = s_in == row
        which = jnp.where((part == 0) & same, 1, which)
        which = jnp.where((part == 2) & same, 2, which)
        which = jnp.where((part == 3) & same, 5, which)
        which = jnp.where((part == 4) & same, 6, which)
        which = jnp.where((part == 1) & (s_in + 1 == row), 3, which)
        which = jnp.where((part == 1) & (s_in == row + 1), 4, which)
        code = jnp.where(which >= 0, which * 8 + g_in, -1)
        middle = jnp.where((part == 1) & same, g_in, -1)
        near, main = [], []
        masks = [[code == (b * 8 + g) for g in range(fields)] for b in range(1, 7)]
        centre = [middle == g for g in range(fields)]
        for f in range(fields):
            acc = jnp.zeros((cs, kk), F32)
            mid = jnp.zeros((cs, kk), F32)
            for g in range(fields):
                mid = jnp.where(centre[g], -RELAX * blocks[r][f, 0, g], mid)
                for b in range(1, 7):
                    acc = jnp.where(masks[b - 1][g], blocks[r][f, b, g], acc)
            near.append(acc)
            main.append(mid)
        hi, lo = split(jnp.concatenate(near + main, axis=0))
        mat[r][pl.ds(0, 2 * nb), :] = hi
        mat[r][pl.ds(2 * nb, 2 * nb), :] = lo

    def clear(r):
        for n in range(2):
            cen[r][n][pl.ds(0, nb), :] = jnp.zeros((nb, ca), BF16)
            cen[r][n][pl.ds((cp + 1) * nb, nb), :] = jnp.zeros((nb, ca), BF16)
            for p in range(cp):
                ext[r][n][pl.ds(p * kx + 2 * nb, 16), :] = jnp.zeros((16, ca), BF16)

    def cell(ref, p):
        return jnp.concatenate([ref[f, pl.ds(p * cs, cs), :] for f in range(fields)], axis=0)

    def store_split(r, k, p):
        new = cell(psi[r][k], p)
        before = jnp.where(wide == 0, 0.0, pltpu.roll(new, 1, 1))
        after = jnp.where(wide == ca - 1, 0.0, pltpu.roll(new, ca - 1, 1))
        for buf, at, value in (
            (cen, (p + 1) * nb, new),
            (ext, p * kx, before),
            (ext, p * kx + nb, after),
        ):
            hi, lo = split(value)
            buf[r][0][pl.ds(at, nb), :] = hi
            buf[r][1][pl.ds(at, nb), :] = lo

    def columns(r, n, p):
        return jnp.concatenate(
            [cen[r][n][pl.ds(p * nb, 3 * nb), :], ext[r][n][pl.ds(p * kx, kx), :]], axis=0
        )

    def interior(r, k):
        for p in range(cp):
            store_split(r, k, p)
        for q in range(cp // 2):
            cells = (2 * q, 2 * q + 1)
            hi = jnp.concatenate([columns(r, 0, p) for p in cells], axis=1)
            lo = jnp.concatenate([columns(r, 1, p) for p in cells], axis=1)
            first = jnp.dot(mat[r][...], hi, preferred_element_type=F32)
            second = jnp.dot(mat[r][pl.ds(0, 2 * nb), :], lo, preferred_element_type=F32)
            both = first[: 2 * nb] + (first[2 * nb :] + second)
            for n, p in enumerate(cells):
                mine = both[:, n * ca : (n + 1) * ca]
                c = coef[r][pl.ds(p * cs, cs), :]
                c = jnp.concatenate([c] * fields, axis=0)
                new = (cell(psi[r][k], p) + mine[nb:]) + c * (cell(rhs[r], p) + mine[:nb])
                for f in range(fields):
                    psi[r][k + 1][f, pl.ds(p * cs, cs), :] = new[f * cs : (f + 1) * cs]

    for c in loads[:2]:
        c.wait()
    for r in range(2):
        pack_span(r, 0)
    for c in loads[2:6]:
        c.wait()
    pack_face(0)
    pl.semaphore_wait(barrier, others)
    start_halos(ROTOR, 0)
    start_face(0)
    start_halos(STATOR, 0)

    for r in range(2):
        clear(r)
        build_matrix(r)
    for c in loads[6:]:
        c.wait()
    for r in range(2):
        coef[r][...] = RELAX / coef[r][...]
    interior(ROTOR, 0)
    interior(STATOR, 0)

    for k in range(ITERS):
        more = k + 1 < ITERS
        receive_halos(ROTOR, k)
        add_halos(ROTOR, k)
        if more:
            pack_span(ROTOR, k + 1)
            start_halos(ROTOR, k + 1)
            pack_face(k + 1)
            start_face(k + 1)
            interior(ROTOR, k + 1)
        receive_halos(STATOR, k)
        add_halos(STATOR, k)
        add_inlet(k)
        if more:
            pack_span(STATOR, k + 1)
            start_halos(STATOR, k + 1)
            interior(STATOR, k + 1)

    for k in range(ITERS):
        for r in range(2):
            finish_sends(r, k)
        sent_faces(k).wait()


def write_out(*refs):
    srcs, dsts, sem = refs[:2], refs[2:4], refs[4]
    copies = [pltpu.make_async_copy(srcs[n], dsts[n], sem.at[n]) for n in range(2)]
    for c in copies:
        c.start()
    for c in copies:
        c.wait()


def per_device(
    npass,
    nspan,
    psi_rotor,
    psi_stator,
    rhs_rotor,
    rhs_stator,
    kappa_rotor,
    kappa_stator,
    rotor_blocks,
    stator_blocks,
    interface_block,
    pass_counts,
    tile_source,
):
    fields, cp, cs, ca = psi_rotor.shape
    shape = (fields, cp * cs, ca)
    flat = [x.reshape(shape) for x in (psi_rotor, psi_stator, rhs_rotor, rhs_stator)]
    kaps = [x.reshape(cp * cs, ca) for x in (kappa_rotor, kappa_stator)]
    small = [x.transpose(1, 0, 2) for x in (rotor_blocks, stator_blocks)]
    small += [interface_block, tile_source]
    nb = fields * cs
    kx = 2 * nb + 16
    state = pltpu.VMEM(shape, F32)
    scratch = [state] * (2 * ITERS)
    scratch += [state] * 2
    scratch += [pltpu.VMEM((cp * cs, ca), F32)] * 2
    scratch += [pltpu.VMEM(((cp + 2) * nb, ca), BF16)] * 4
    scratch += [pltpu.VMEM((cp * kx, ca), BF16)] * 4
    scratch += [pltpu.VMEM((4 * nb, 5 * nb + 16), BF16)] * 2
    scratch += [pltpu.SMEM(x.shape, x.dtype) for x in small]
    scratch += [
        pltpu.VMEM((2, ITERS, 2, fields, cs, ca), F32),
        pltpu.VMEM((2, ITERS, 2, fields, cp, ca), F32),
        pltpu.VMEM((2, ITERS, 2, fields, cp, ca), F32),
        pltpu.VMEM((ITERS, 1, ca), F32),
    ]
    scratch += [pltpu.VMEM((npass * nspan, 1, ca), F32)] * ITERS
    dma = pltpu.SemaphoreType.DMA
    scratch += [
        dma((10,)),
        dma((2, ITERS, 4)),
        dma((2, ITERS, 4)),
        dma((ITERS,)),
        dma((ITERS,)),
    ]
    hbm = pl.BlockSpec(memory_space=pltpu.HBM)
    vmem = pl.BlockSpec(memory_space=pltpu.VMEM)
    done = pl.pallas_call(
        functools.partial(kernel, fields, cp, cs, ca, npass, nspan),
        out_shape=[pltpu.VMEM(shape, F32)] * 2,
        in_specs=[hbm] * 10 + [pl.BlockSpec(memory_space=pltpu.SMEM)],
        out_specs=[vmem] * 2,
        scratch_shapes=scratch,
        compiler_params=pltpu.CompilerParams(
            collective_id=0, has_side_effects=True, vmem_limit_bytes=32 * 1024 * 1024
        ),
    )(*[pltpu.with_memory_space_constraint(x, pltpu.HBM) for x in flat + kaps + small], pass_counts)
    out = pl.pallas_call(
        write_out,
        out_shape=[pltpu.HBM(shape, F32)] * 2,
        in_specs=[vmem] * 2,
        out_specs=[hbm] * 2,
        scratch_shapes=[dma((2,))],
    )(*[pltpu.with_memory_space_constraint(x, pltpu.VMEM) for x in done])
    return tuple(x.reshape(psi_rotor.shape) for x in out)


def solution(mesh):
    return jax.shard_map(
        functools.partial(per_device, mesh.shape["passage"], mesh.shape["span"]),
        mesh=mesh,
        in_specs=(
            P(None, "passage", "span", None),
            P(None, "passage", "span", None),
            P(None, "passage", "span", None),
            P(None, "passage", "span", None),
            P("passage", "span", None),
            P("passage", "span", None),
            P(),
            P(),
            P(),
            P("passage"),
            P(),
        ),
        out_specs=(P(None, "passage", "span", None), P(None, "passage", "span", None)),
        check_vma=False,
    )
```

```python
import functools

import jax
import jax.numpy as jnp
from jax import lax
from jax.experimental import pallas as pl
from jax.experimental.pallas import tpu as pltpu
from jax.sharding import PartitionSpec as P

ITERS = 3
RELAX = 0.8
MESH = pl.DeviceIdType.MESH
F32 = jnp.float32
BF16 = jnp.bfloat16
ROTOR, STATOR = 0, 1
SLOT = 16


def split(x):
    hi = x.astype(BF16)
    lo = (x - hi.astype(F32)).astype(BF16)
    return hi, lo


def kernel(fields, cp, cs, ca, npass, nspan, *refs):
    it = iter(refs)

    def take(n):
        return [next(it) for _ in range(n)]

    psi_in = take(2)
    rhs_in = take(2)
    kap_in = take(2)
    small_in = take(4)
    (counts,) = take(1)
    outs = take(2)
    psi = [take(ITERS) + [outs[r]] for r in range(2)]
    rhs = take(2)
    coef = take(2)
    cen = [take(2) for _ in range(2)]
    ext = [take(2) for _ in range(2)]
    mat = take(2)
    small = take(4)
    blocks, (iface, source) = small[:2], small[2:]
    (precv, psend, ssend, srecv, fsend, pcor, scor) = take(7)
    frecv = take(ITERS)
    (in_sem, hs_sem, hr_sem, fs_sem, fr_sem, gate) = take(6)

    nb = fields * cs
    kx = 2 * nb + 16
    plane = cp * cs
    others = npass * nspan - 1

    ip = lax.axis_index("passage")
    js = lax.axis_index("span")
    right = lax.rem(ip + 1, npass)
    left = lax.rem(ip + npass - 1, npass)
    has_next, has_prev = js < nspan - 1, js > 0

    def peer(o):
        return lax.rem(ip + o // nspan, npass), lax.rem(js + o % nspan, nspan)

    def each_peer(body):
        unroll = others if others < 64 else 1
        pl.loop(1, others + 1, unroll=unroll)(body)

    pairs = [
        (psi_in[0], psi[0][0]),
        (psi_in[1], psi[1][0].at[pl.ds(0, fields)]),
        (kap_in[1], psi[STATOR][0].at[fields]),
        *zip(small_in, small),
        (kap_in[0], coef[0]),
        (rhs_in[0], rhs[0]),
        (rhs_in[1], rhs[1]),
    ]
    loads = [pltpu.make_async_copy(a, b, in_sem.at[n]) for n, (a, b) in enumerate(pairs)]
    for c in loads:
        c.start()

    barrier = pltpu.get_barrier_semaphore()
    for o in range(1, npass):
        pl.semaphore_signal(
            barrier, inc=1, device_id=(lax.rem(ip + o, npass), js), device_id_type=MESH
        )
    for o in range(1, nspan):
        pl.semaphore_signal(
            barrier, inc=1, device_id=(ip, lax.rem(js + o, nspan)), device_id_type=MESH
        )

    for d, met in ((0, has_prev), (1, has_next)):

        @pl.when(jnp.logical_not(met))
        def _(d=d):
            for r in range(2):
                for k in range(ITERS):
                    srecv[r, k, d, pl.ds(0, fields)] = jnp.zeros((fields, cp, ca), F32)
                    srecv[r, k, d, fields] = jnp.ones((cp, ca), F32)

    def halo_copies(r, k):
        made = []
        n = fields + 1 if (r, k) == (STATOR, 0) else fields
        for d, p, target in ((0, cp - 1, (right, js)), (1, 0, (left, js))):
            made.append(
                pltpu.make_async_remote_copy(
                    src_ref=psend.at[d]
                    if (r, k) == (STATOR, 1)
                    else psi[r][k].at[:, pl.ds(p * cs, cs), :],
                    dst_ref=precv.at[r, k, d, pl.ds(0, n)],
                    send_sem=hs_sem.at[r, k, d],
                    recv_sem=hr_sem.at[r, k, d],
                    device_id=target,
                    device_id_type=MESH,
                )
            )
        for d, target in (
            (0, (ip, lax.rem(js + 1, nspan))),
            (1, (ip, lax.rem(js + nspan - 1, nspan))),
        ):
            made.append(
                pltpu.make_async_remote_copy(
                    src_ref=ssend.at[r, k, d, pl.ds(0, n)],
                    dst_ref=srecv.at[r, k, d, pl.ds(0, n)],
                    send_sem=hs_sem.at[r, k, 2 + d],
                    recv_sem=hr_sem.at[r, k, 2 + d],
                    device_id=target,
                    device_id_type=MESH,
                )
            )
        return made

    halos = {(r, k): halo_copies(r, k) for r in range(2) for k in range(ITERS)}

    def edge(s):
        return pl.ds(s, cp, stride=cs)

    def pack_span(r, k):
        for d, s in ((0, cs - 1), (1, 0)):
            for f in range(psi[r][k].shape[0]):
                ssend[r, k, d, f] = psi[r][k][f, edge(s), :]

    def pack_pitch(r, k):
        for d, p in ((0, cp - 1), (1, 0)):
            for f in range(fields):
                psend[d, f] = psi[r][k][f, pl.ds(p * cs, cs), :]

    def start_halos(r, k):
        to_right, to_left, to_next, to_prev = halos[r, k]
        to_right.start()
        to_left.start()

        @pl.when(has_next)
        def _():
            to_next.start()

        @pl.when(has_prev)
        def _():
            to_prev.start()

    def finish_sends(r, k):
        to_right, to_left, to_next, to_prev = halos[r, k]
        to_right.wait_send()
        to_left.wait_send()

        @pl.when(has_next)
        def _():
            to_next.wait_send()

        @pl.when(has_prev)
        def _():
            to_prev.wait_send()

    def receive_halos(r, k):
        to_right, to_left, to_next, to_prev = halos[r, k]

        @pl.when(has_prev)
        def _():
            to_next.wait_recv()

        @pl.when(has_next)
        def _():
            to_prev.wait_recv()

        to_right.wait_recv()
        to_left.wait_recv()

    def mix(block, f, parts):
        acc = block(f, 0) * parts[0]
        for g in range(1, fields):
            acc = acc + block(f, g) * parts[g]
        return acc

    def add_halos(r, k):
        new = psi[r][k + 1]
        for d, p in ((0, 0), (1, cp - 1)):
            rows = pl.ds(p * cs, cs)
            c = coef[r][rows, :]
            parts = [precv[r, k, d, g] for g in range(fields)]
            if (r, k) == (STATOR, 1):
                parts = [x + pcor[d, g] for g, x in enumerate(parts)]
            for f in range(fields):
                acc = mix(lambda a, b: blocks[r][a, 1 + d, b], f, parts)
                new[f, rows, :] = new[f, rows, :] + c * acc
        for d, s in ((0, 0), (1, cs - 1)):
            c = coef[r][edge(s), :]
            parts = [srecv[r, k, d, g] for g in range(fields)]
            if (r, k) == (STATOR, 1):
                parts = [x + scor[d, g] for g, x in enumerate(parts)]
            for f in range(fields):
                acc = mix(lambda a, b: blocks[r][a, 3 + d, b], f, parts)
                new[f, edge(s), :] = new[f, edge(s), :] + c * acc

    lane = lax.broadcasted_iota(jnp.int32, (cs, ca), 1)
    at_slot = lane - SLOT * lax.broadcasted_iota(jnp.int32, (cs, ca), 0)
    wide = lax.broadcasted_iota(jnp.int32, (nb, ca), 1)

    def face_copy(k, o):
        return pltpu.make_async_remote_copy(
            src_ref=fsend.at[k],
            dst_ref=frecv[k].at[o],
            send_sem=fs_sem.at[k],
            recv_sem=fr_sem.at[k],
            device_id=peer(o),
            device_id_type=MESH,
        )

    def pick(x):
        return jnp.sum(x, axis=1, keepdims=True)

    def pack_face(k):
        state = psi[ROTOR][k]
        count = counts[0]
        weights = [jnp.where(p < count, 1.0, 0.0).astype(F32) for p in range(cp)]
        sums = []
        for f in range(fields):
            acc = weights[0] * state[f, pl.ds(0, cs), :]
            for p in range(1, cp):
                acc = acc + weights[p] * state[f, pl.ds(p * cs, cs), :]
            sums.append(jnp.where(lane == ca - 1, acc, 0.0))
        tile = jnp.where(at_slot == fields, jnp.clip(count, 0, cp).astype(F32), 0.0)
        for f in range(fields):
            mixed = mix(lambda a, b: iface[a, b], f, sums)
            tile = jnp.where(at_slot == f, pick(mixed), tile)
        row = jnp.sum(tile, axis=0, keepdims=True)
        fsend[k] = row
        frecv[k][0] = row

    def start_face(k):
        each_peer(lambda o: face_copy(k, o).start())

    def all_faces(k):
        return pltpu.make_async_copy(
            frecv[k].at[pl.ds(1, others)], frecv[k].at[pl.ds(1, others)], fr_sem.at[k]
        )

    def sent_faces(k):
        return pltpu.make_async_copy(
            frecv[k].at[pl.ds(1, others)], frecv[k].at[pl.ds(1, others)], fs_sem.at[k]
        )

    def inlets(k, at):
        away = lax.rem(js - source[at] + nspan, nspan)
        total = frecv[k][away]
        for o in range(1, npass):
            total = total + frecv[k][o * nspan + away]
        total = jnp.broadcast_to(total, (cs, ca))
        count = pick(jnp.where(at_slot == fields, total, 0.0))
        made = []
        for f in range(fields):
            value = pick(jnp.where(at_slot == f, total, 0.0)) / count
            made.append(jnp.where(lane == 0, value, 0.0))
        return made

    def add_inlet(k):
        all_faces(k).wait()
        new = psi[STATOR][k + 1]
        values = inlets(k, js)
        for f in range(fields):
            for p in range(cp):
                rows = pl.ds(p * cs, cs)
                new[f, rows, :] = new[f, rows, :] + coef[STATOR][rows, :] * values[f]
        return values

    def neighbour_inlets(own):
        for d in range(2):
            c = RELAX / precv[STATOR, 0, d, fields]
            for f in range(fields):
                pcor[d, f] = c * own[f]
        for d, s, at, met in (
            (0, cs - 1, jnp.maximum(js - 1, 0), has_prev),
            (1, 0, jnp.minimum(js + 1, nspan - 1), has_next),
        ):
            c = jnp.where(met, 1.0, 0.0) * (RELAX / srecv[STATOR, 0, d, fields])
            values = inlets(0, at)
            for f in range(fields):
                scor[d, f] = c * jnp.broadcast_to(values[f][s : s + 1], (cp, ca))

    def build_matrix(r):
        kk = 5 * nb + 16
        col = lax.broadcasted_iota(jnp.int32, (cs, kk), 1)
        row = lax.broadcasted_iota(jnp.int32, (cs, kk), 0)
        part = col // nb
        g_in = (col - part * nb) // cs
        s_in = col - part * nb - g_in * cs
        which = jnp.full((cs, kk), -1, jnp.int32)
        same = s_in == row
        which = jnp.where((part == 0) & same, 1, which)
        which = jnp.where((part == 2) & same, 2, which)
        which = jnp.where((part == 3) & same, 5, which)
        which = jnp.where((part == 4) & same, 6, which)
        which = jnp.where((part == 1) & (s_in + 1 == row), 3, which)
        which = jnp.where((part == 1) & (s_in == row + 1), 4, which)
        code = jnp.where(which >= 0, which * 8 + g_in, -1)
        middle = jnp.where((part == 1) & same, g_in, -1)
        near, main = [], []
        masks = [[code == (b * 8 + g) for g in range(fields)] for b in range(1, 7)]
        centre = [middle == g for g in range(fields)]
        for f in range(fields):
            acc = jnp.zeros((cs, kk), F32)
            mid = jnp.zeros((cs, kk), F32)
            for g in range(fields):
                mid = jnp.where(centre[g], -RELAX * blocks[r][f, 0, g], mid)
                for b in range(1, 7):
                    acc = jnp.where(masks[b - 1][g], blocks[r][f, b, g], acc)
            near.append(acc)
            main.append(mid)
        hi, lo = split(jnp.concatenate(near + main, axis=0))
        mat[r][pl.ds(0, 2 * nb), :] = hi
        mat[r][pl.ds(2 * nb, 2 * nb), :] = lo

    def clear(r):
        for n in range(2):
            cen[r][n][pl.ds(0, nb), :] = jnp.zeros((nb, ca), BF16)
            cen[r][n][pl.ds((cp + 1) * nb, nb), :] = jnp.zeros((nb, ca), BF16)
            for p in range(cp):
                ext[r][n][pl.ds(p * kx + 2 * nb, 16), :] = jnp.zeros((16, ca), BF16)

    def cell(ref, p):
        return jnp.concatenate([ref[f, pl.ds(p * cs, cs), :] for f in range(fields)], axis=0)

    def store_split(r, k, p):
        new = cell(psi[r][k], p)
        before = jnp.where(wide == 0, 0.0, pltpu.roll(new, 1, 1))
        after = jnp.where(wide == ca - 1, 0.0, pltpu.roll(new, ca - 1, 1))
        for buf, at, value in (
            (cen, (p + 1) * nb, new),
            (ext, p * kx, before),
            (ext, p * kx + nb, after),
        ):
            hi, lo = split(value)
            buf[r][0][pl.ds(at, nb), :] = hi
            buf[r][1][pl.ds(at, nb), :] = lo

    def columns(r, n, p):
        return jnp.concatenate(
            [cen[r][n][pl.ds(p * nb, 3 * nb), :], ext[r][n][pl.ds(p * kx, kx), :]], axis=0
        )

    def interior(r, k):
        for p in range(cp):
            store_split(r, k, p)
        for q in range(cp // 2):
            cells = (2 * q, 2 * q + 1)
            hi = jnp.concatenate([columns(r, 0, p) for p in cells], axis=1)
            lo = jnp.concatenate([columns(r, 1, p) for p in cells], axis=1)
            first = jnp.dot(mat[r][...], hi, preferred_element_type=F32)
            second = jnp.dot(mat[r][pl.ds(0, 2 * nb), :], lo, preferred_element_type=F32)
            both = first[: 2 * nb] + (first[2 * nb :] + second)
            for n, p in enumerate(cells):
                mine = both[:, n * ca : (n + 1) * ca]
                c = coef[r][pl.ds(p * cs, cs), :]
                c = jnp.concatenate([c] * fields, axis=0)
                new = (cell(psi[r][k], p) + mine[nb:]) + c * (cell(rhs[r], p) + mine[:nb])
                for f in range(fields):
                    psi[r][k + 1][f, pl.ds(p * cs, cs), :] = new[f * cs : (f + 1) * cs]

    loads[0].wait()
    pack_span(ROTOR, 0)
    pl.semaphore_wait(barrier, npass + nspan - 2)
    start_halos(ROTOR, 0)
    for o in range(1, npass):
        pl.semaphore_signal(
            gate, inc=1, device_id=(lax.rem(ip + o, npass), js), device_id_type=MESH
        )
    for c in loads[1:3]:
        c.wait()
    pack_span(STATOR, 0)
    start_halos(STATOR, 0)
    for c in loads[3:7]:
        c.wait()
    pack_face(0)
    pl.semaphore_wait(gate, npass - 1)
    start_face(0)

    for r in range(2):
        clear(r)
        build_matrix(r)
    for c in loads[7:]:
        c.wait()
    coef[ROTOR][...] = RELAX / coef[ROTOR][...]
    coef[STATOR][...] = RELAX / psi[STATOR][0][fields]
    interior(ROTOR, 0)
    interior(STATOR, 0)

    receive_halos(ROTOR, 0)
    add_halos(ROTOR, 0)
    pack_span(ROTOR, 1)
    start_halos(ROTOR, 1)
    pack_face(1)
    start_face(1)
    receive_halos(STATOR, 0)
    add_halos(STATOR, 0)
    pack_span(STATOR, 1)
    pack_pitch(STATOR, 1)
    start_halos(STATOR, 1)
    interior(ROTOR, 1)

    receive_halos(ROTOR, 1)
    add_halos(ROTOR, 1)
    pack_face(2)
    start_face(2)
    pack_span(ROTOR, 2)
    start_halos(ROTOR, 2)
    own = add_inlet(0)
    neighbour_inlets(own)
    interior(STATOR, 1)
    receive_halos(STATOR, 1)
    add_halos(STATOR, 1)
    add_inlet(1)
    pack_span(STATOR, 2)
    start_halos(STATOR, 2)
    interior(ROTOR, 2)
    interior(STATOR, 2)

    receive_halos(ROTOR, 2)
    add_halos(ROTOR, 2)
    receive_halos(STATOR, 2)
    add_halos(STATOR, 2)
    add_inlet(2)

    for k in range(ITERS):
        for r in range(2):
            finish_sends(r, k)
        sent_faces(k).wait()


def write_out(*refs):
    srcs, dsts, sem = refs[:2], refs[2:4], refs[4]
    copies = [pltpu.make_async_copy(srcs[n], dsts[n], sem.at[n]) for n in range(2)]
    for c in copies:
        c.start()
    for c in copies:
        c.wait()


def per_device(
    npass,
    nspan,
    psi_rotor,
    psi_stator,
    rhs_rotor,
    rhs_stator,
    kappa_rotor,
    kappa_stator,
    rotor_blocks,
    stator_blocks,
    interface_block,
    pass_counts,
    tile_source,
):
    fields, cp, cs, ca = psi_rotor.shape
    shape = (fields, cp * cs, ca)
    flat = [x.reshape(shape) for x in (psi_rotor, psi_stator, rhs_rotor, rhs_stator)]
    kaps = [x.reshape(cp * cs, ca) for x in (kappa_rotor, kappa_stator)]
    small = [x.transpose(1, 0, 2) for x in (rotor_blocks, stator_blocks)]
    small += [interface_block, tile_source]
    nb = fields * cs
    kx = 2 * nb + 16
    state = pltpu.VMEM(shape, F32)
    scratch = [state] * ITERS
    scratch += [pltpu.VMEM((fields + 1, cp * cs, ca), F32)]
    scratch += [state] * (ITERS - 1)
    scratch += [state] * 2
    scratch += [pltpu.VMEM((cp * cs, ca), F32)] * 2
    scratch += [pltpu.VMEM(((cp + 2) * nb, ca), BF16)] * 4
    scratch += [pltpu.VMEM((cp * kx, ca), BF16)] * 4
    scratch += [pltpu.VMEM((4 * nb, 5 * nb + 16), BF16)] * 2
    scratch += [pltpu.SMEM(x.shape, x.dtype) for x in small]
    scratch += [
        pltpu.VMEM((2, ITERS, 2, fields + 1, cs, ca), F32),
        pltpu.VMEM((2, fields, cs, ca), F32),
        pltpu.VMEM((2, ITERS, 2, fields + 1, cp, ca), F32),
        pltpu.VMEM((2, ITERS, 2, fields + 1, cp, ca), F32),
        pltpu.VMEM((ITERS, 1, ca), F32),
        pltpu.VMEM((2, fields, cs, ca), F32),
        pltpu.VMEM((2, fields, cp, ca), F32),
    ]
    scratch += [pltpu.VMEM((npass * nspan, 1, ca), F32)] * ITERS
    dma = pltpu.SemaphoreType.DMA
    scratch += [
        dma((10,)),
        dma((2, ITERS, 4)),
        dma((2, ITERS, 4)),
        dma((ITERS,)),
        dma((ITERS,)),
        pltpu.SemaphoreType.REGULAR,
    ]
    hbm = pl.BlockSpec(memory_space=pltpu.HBM)
    vmem = pl.BlockSpec(memory_space=pltpu.VMEM)
    done = pl.pallas_call(
        functools.partial(kernel, fields, cp, cs, ca, npass, nspan),
        out_shape=[pltpu.VMEM(shape, F32)] * 2,
        in_specs=[hbm] * 10 + [pl.BlockSpec(memory_space=pltpu.SMEM)],
        out_specs=[vmem] * 2,
        scratch_shapes=scratch,
        compiler_params=pltpu.CompilerParams(
            collective_id=0, has_side_effects=True, vmem_limit_bytes=32 * 1024 * 1024
        ),
    )(*[pltpu.with_memory_space_constraint(x, pltpu.HBM) for x in flat + kaps + small], pass_counts)
    out = pl.pallas_call(
        write_out,
        out_shape=[pltpu.HBM(shape, F32)] * 2,
        in_specs=[vmem] * 2,
        out_specs=[hbm] * 2,
        scratch_shapes=[dma((2,))],
    )(*[pltpu.with_memory_space_constraint(x, pltpu.VMEM) for x in done])
    return tuple(x.reshape(psi_rotor.shape) for x in out)


def solution(mesh):
    return jax.shard_map(
        functools.partial(per_device, mesh.shape["passage"], mesh.shape["span"]),
        mesh=mesh,
        in_specs=(
            P(None, "passage", "span", None),
            P(None, "passage", "span", None),
            P(None, "passage", "span", None),
            P(None, "passage", "span", None),
            P("passage", "span", None),
            P("passage", "span", None),
            P(),
            P(),
            P(),
            P("passage"),
            P(),
        ),
        out_specs=(P(None, "passage", "span", None), P(None, "passage", "span", None)),
        check_vma=False,
    )
```

```python
import functools

import jax
import jax.numpy as jnp
from jax import lax
from jax.experimental import pallas as pl
from jax.experimental.pallas import tpu as pltpu
from jax.sharding import PartitionSpec as P

ITERS = 3
RELAX = 0.8
MESH = pl.DeviceIdType.MESH
F32 = jnp.float32
BF16 = jnp.bfloat16
ROTOR, STATOR = 0, 1
SLOT = 16


def split(x):
    hi = x.astype(BF16)
    lo = (x - hi.astype(F32)).astype(BF16)
    return hi, lo


def kernel(fields, cp, cs, ca, npass, nspan, *refs):
    it = iter(refs)

    def take(n):
        return [next(it) for _ in range(n)]

    psi_in = take(2)
    rhs_in = take(2)
    kap_in = take(2)
    small_in = take(4)
    (counts,) = take(1)
    outs = take(2)
    psi = [take(ITERS) + [outs[r]] for r in range(2)]
    rhs = take(2)
    coef = take(2)
    cen = [take(2) for _ in range(2)]
    ext = [take(2) for _ in range(2)]
    mat = take(2)
    small = take(4)
    blocks, (iface, source) = small[:2], small[2:]
    (precv, psend, ssend, srecv, fsend, pcor, scor) = take(7)
    frecv = take(ITERS)
    (in_sem, hs_sem, hr_sem, fs_sem, fr_sem, gate) = take(6)

    nb = fields * cs
    kx = 2 * nb + 16
    plane = cp * cs
    others = npass * nspan - 1

    ip = lax.axis_index("passage")
    js = lax.axis_index("span")
    right = lax.rem(ip + 1, npass)
    left = lax.rem(ip + npass - 1, npass)
    has_next, has_prev = js < nspan - 1, js > 0

    def peer(o):
        return lax.rem(ip + o // nspan, npass), lax.rem(js + o % nspan, nspan)

    def each_peer(body):
        unroll = others if others < 64 else 1
        pl.loop(1, others + 1, unroll=unroll)(body)

    pairs = [
        (psi_in[0], psi[0][0]),
        (psi_in[1], psi[1][0].at[pl.ds(0, fields)]),
        (kap_in[1], psi[STATOR][0].at[fields]),
        *zip(small_in, small),
        (kap_in[0], coef[0]),
        (rhs_in[0], rhs[0]),
        (rhs_in[1], rhs[1]),
    ]
    loads = [pltpu.make_async_copy(a, b, in_sem.at[n]) for n, (a, b) in enumerate(pairs)]
    for c in loads:
        c.start()

    barrier = pltpu.get_barrier_semaphore()
    for o in range(1, npass):
        pl.semaphore_signal(
            barrier, inc=1, device_id=(lax.rem(ip + o, npass), js), device_id_type=MESH
        )
    for o in range(1, nspan):
        pl.semaphore_signal(
            barrier, inc=1, device_id=(ip, lax.rem(js + o, nspan)), device_id_type=MESH
        )

    for d, met in ((0, has_prev), (1, has_next)):

        @pl.when(jnp.logical_not(met))
        def _(d=d):
            for r in range(2):
                for k in range(ITERS):
                    srecv[r, k, d, pl.ds(0, fields)] = jnp.zeros((fields, cp, ca), F32)
                    srecv[r, k, d, fields] = jnp.ones((cp, ca), F32)

    def halo_copies(r, k):
        made = []
        n = fields + 1 if (r, k) == (STATOR, 0) else fields
        for d, p, target in ((0, cp - 1, (right, js)), (1, 0, (left, js))):
            made.append(
                pltpu.make_async_remote_copy(
                    src_ref=psend.at[d]
                    if (r, k) == (STATOR, 1)
                    else psi[r][k].at[:, pl.ds(p * cs, cs), :],
                    dst_ref=precv.at[r, k, d, pl.ds(0, n)],
                    send_sem=hs_sem.at[r, k, d],
                    recv_sem=hr_sem.at[r, k, d],
                    device_id=target,
                    device_id_type=MESH,
                )
            )
        for d, target in (
            (0, (ip, lax.rem(js + 1, nspan))),
            (1, (ip, lax.rem(js + nspan - 1, nspan))),
        ):
            made.append(
                pltpu.make_async_remote_copy(
                    src_ref=ssend.at[r, k, d, pl.ds(0, n)],
                    dst_ref=srecv.at[r, k, d, pl.ds(0, n)],
                    send_sem=hs_sem.at[r, k, 2 + d],
                    recv_sem=hr_sem.at[r, k, 2 + d],
                    device_id=target,
                    device_id_type=MESH,
                )
            )
        return made

    halos = {(r, k): halo_copies(r, k) for r in range(2) for k in range(ITERS)}

    def edge(s):
        return pl.ds(s, cp, stride=cs)

    def pack_span(r, k):
        for d, s in ((0, cs - 1), (1, 0)):
            for f in range(psi[r][k].shape[0]):
                ssend[r, k, d, f] = psi[r][k][f, edge(s), :]

    def start_pitch(r, k):
        to_right, to_left = halos[r, k][:2]

        @pl.when(ip == 0)
        def _():
            to_left.start()
            to_right.start()

        @pl.when(ip > 0)
        def _():
            to_right.start()
            to_left.start()

    def start_far(r, k):
        to_right, to_left = halos[r, k][:2]

        @pl.when(ip == 0)
        def _():
            to_left.start()

        @pl.when(ip > 0)
        def _():
            to_right.start()

    def start_near(r, k):
        to_right, to_left = halos[r, k][:2]

        @pl.when(ip == 0)
        def _():
            to_right.start()

        @pl.when(ip > 0)
        def _():
            to_left.start()

    def start_span(r, k):
        to_next, to_prev = halos[r, k][2:]

        @pl.when(has_next)
        def _():
            to_next.start()

        @pl.when(has_prev)
        def _():
            to_prev.start()

    def finish_sends(r, k):
        to_right, to_left, to_next, to_prev = halos[r, k]
        to_right.wait_send()
        to_left.wait_send()

        @pl.when(has_next)
        def _():
            to_next.wait_send()

        @pl.when(has_prev)
        def _():
            to_prev.wait_send()

    def mix(block, f, parts):
        acc = block(f, 0) * parts[0]
        for g in range(1, fields):
            acc = acc + block(f, g) * parts[g]
        return acc

    def span_terms(r, k):
        new = psi[r][k + 1]
        to_next, to_prev = halos[r, k][2:]

        @pl.when(has_prev)
        def _():
            to_next.wait_recv()

        @pl.when(has_next)
        def _():
            to_prev.wait_recv()

        for d, s in ((0, 0), (1, cs - 1)):
            c = coef[r][edge(s), :]
            parts = [srecv[r, k, d, g] for g in range(fields)]
            if (r, k) == (STATOR, 1):
                parts = [x + scor[d, g] for g, x in enumerate(parts)]
            for f in range(fields):
                acc = mix(lambda a, b: blocks[r][a, 3 + d, b], f, parts)
                new[f, edge(s), :] = new[f, edge(s), :] + c * acc

    def add_halos(r, k, send):
        span_terms(r, k)
        new = psi[r][k + 1]
        for d, p in ((0, 0), (1, cp - 1)):
            rows = pl.ds(p * cs, cs)
            c = coef[r][rows, :]
            halos[r, k][d].wait_recv()
            parts = [precv[r, k, d, g] for g in range(fields)]
            if (r, k) == (STATOR, 1):
                parts = [x + pcor[d, g] for g, x in enumerate(parts)]
            for f in range(fields):
                acc = mix(lambda a, b: blocks[r][a, 1 + d, b], f, parts)
                value = new[f, rows, :] + c * acc
                new[f, rows, :] = value
                if send and (r, k) == (STATOR, 0):
                    psend[1 - d, f] = value
            if send:
                halos[r, k + 1][1 - d].start()
        if send:
            pack_span(r, k + 1)
            start_span(r, k + 1)

    lane = lax.broadcasted_iota(jnp.int32, (cs, ca), 1)
    at_slot = lane - SLOT * lax.broadcasted_iota(jnp.int32, (cs, ca), 0)
    wide = lax.broadcasted_iota(jnp.int32, (nb, ca), 1)

    def face_copy(k, o):
        return pltpu.make_async_remote_copy(
            src_ref=fsend.at[k],
            dst_ref=frecv[k].at[o],
            send_sem=fs_sem.at[k],
            recv_sem=fr_sem.at[k],
            device_id=peer(o),
            device_id_type=MESH,
        )

    def pick(x):
        return jnp.sum(x, axis=1, keepdims=True)

    def pack_face(k):
        state = psi[ROTOR][k]
        count = counts[0]
        weights = [jnp.where(p < count, 1.0, 0.0).astype(F32) for p in range(cp)]
        sums = []
        for f in range(fields):
            acc = weights[0] * state[f, pl.ds(0, cs), :]
            for p in range(1, cp):
                acc = acc + weights[p] * state[f, pl.ds(p * cs, cs), :]
            sums.append(jnp.where(lane == ca - 1, acc, 0.0))
        tile = jnp.where(at_slot == fields, jnp.clip(count, 0, cp).astype(F32), 0.0)
        for f in range(fields):
            mixed = mix(lambda a, b: iface[a, b], f, sums)
            tile = jnp.where(at_slot == f, pick(mixed), tile)
        row = jnp.sum(tile, axis=0, keepdims=True)
        fsend[k] = row
        frecv[k][0] = row

    def start_face(k):
        each_peer(lambda o: face_copy(k, o).start())

    def all_faces(k):
        return pltpu.make_async_copy(
            frecv[k].at[pl.ds(1, others)], frecv[k].at[pl.ds(1, others)], fr_sem.at[k]
        )

    def sent_faces(k):
        return pltpu.make_async_copy(
            frecv[k].at[pl.ds(1, others)], frecv[k].at[pl.ds(1, others)], fs_sem.at[k]
        )

    def inlets(k, at):
        away = lax.rem(js - source[at] + nspan, nspan)
        total = frecv[k][away]
        for o in range(1, npass):
            total = total + frecv[k][o * nspan + away]
        total = jnp.broadcast_to(total, (cs, ca))
        count = pick(jnp.where(at_slot == fields, total, 0.0))
        made = []
        for f in range(fields):
            value = pick(jnp.where(at_slot == f, total, 0.0)) / count
            made.append(jnp.where(lane == 0, value, 0.0))
        return made

    def add_inlet(k, send):
        all_faces(k).wait()
        new = psi[STATOR][k + 1]
        values = inlets(k, js)

        def add(p):
            rows = pl.ds(p * cs, cs)
            for f in range(fields):
                new[f, rows, :] = new[f, rows, :] + coef[STATOR][rows, :] * values[f]

        add(0)
        add(cp - 1)
        if send:
            start_pitch(STATOR, k + 1)
        for p in range(1, cp - 1):
            add(p)
        if send:
            pack_span(STATOR, k + 1)
            start_span(STATOR, k + 1)
        return values

    def neighbour_inlets(own):
        for d in range(2):
            c = RELAX / precv[STATOR, 0, d, fields]
            for f in range(fields):
                pcor[d, f] = c * own[f]
        for d, s, at, met in (
            (0, cs - 1, jnp.maximum(js - 1, 0), has_prev),
            (1, 0, jnp.minimum(js + 1, nspan - 1), has_next),
        ):
            c = jnp.where(met, 1.0, 0.0) * (RELAX / srecv[STATOR, 0, d, fields])
            values = inlets(0, at)
            for f in range(fields):
                scor[d, f] = c * jnp.broadcast_to(values[f][s : s + 1], (cp, ca))

    def build_matrix(r):
        kk = 5 * nb + 16
        col = lax.broadcasted_iota(jnp.int32, (cs, kk), 1)
        row = lax.broadcasted_iota(jnp.int32, (cs, kk), 0)
        part = col // nb
        g_in = (col - part * nb) // cs
        s_in = col - part * nb - g_in * cs
        which = jnp.full((cs, kk), -1, jnp.int32)
        same = s_in == row
        which = jnp.where((part == 0) & same, 1, which)
        which = jnp.where((part == 2) & same, 2, which)
        which = jnp.where((part == 3) & same, 5, which)
        which = jnp.where((part == 4) & same, 6, which)
        which = jnp.where((part == 1) & (s_in + 1 == row), 3, which)
        which = jnp.where((part == 1) & (s_in == row + 1), 4, which)
        code = jnp.where(which >= 0, which * 8 + g_in, -1)
        middle = jnp.where((part == 1) & same, g_in, -1)
        near, main = [], []
        masks = [[code == (b * 8 + g) for g in range(fields)] for b in range(1, 7)]
        centre = [middle == g for g in range(fields)]
        for f in range(fields):
            acc = jnp.zeros((cs, kk), F32)
            mid = jnp.zeros((cs, kk), F32)
            for g in range(fields):
                mid = jnp.where(centre[g], -RELAX * blocks[r][f, 0, g], mid)
                for b in range(1, 7):
                    acc = jnp.where(masks[b - 1][g], blocks[r][f, b, g], acc)
            near.append(acc)
            main.append(mid)
        hi, lo = split(jnp.concatenate(near + main, axis=0))
        mat[r][pl.ds(0, 2 * nb), :] = hi
        mat[r][pl.ds(2 * nb, 2 * nb), :] = lo

    def clear(r):
        for n in range(2):
            cen[r][n][pl.ds(0, nb), :] = jnp.zeros((nb, ca), BF16)
            cen[r][n][pl.ds((cp + 1) * nb, nb), :] = jnp.zeros((nb, ca), BF16)
            for p in range(cp):
                ext[r][n][pl.ds(p * kx + 2 * nb, 16), :] = jnp.zeros((16, ca), BF16)

    def cell(ref, p):
        return jnp.concatenate([ref[f, pl.ds(p * cs, cs), :] for f in range(fields)], axis=0)

    def store_split(r, k, p):
        new = cell(psi[r][k], p)
        before = jnp.where(wide == 0, 0.0, pltpu.roll(new, 1, 1))
        after = jnp.where(wide == ca - 1, 0.0, pltpu.roll(new, ca - 1, 1))
        for buf, at, value in (
            (cen, (p + 1) * nb, new),
            (ext, p * kx, before),
            (ext, p * kx + nb, after),
        ):
            hi, lo = split(value)
            buf[r][0][pl.ds(at, nb), :] = hi
            buf[r][1][pl.ds(at, nb), :] = lo

    def columns(r, n, p):
        return jnp.concatenate(
            [cen[r][n][pl.ds(p * nb, 3 * nb), :], ext[r][n][pl.ds(p * kx, kx), :]], axis=0
        )

    def interior(r, k):
        for p in range(cp):
            store_split(r, k, p)
        for q in range(cp // 2):
            cells = (2 * q, 2 * q + 1)
            hi = jnp.concatenate([columns(r, 0, p) for p in cells], axis=1)
            lo = jnp.concatenate([columns(r, 1, p) for p in cells], axis=1)
            first = jnp.dot(mat[r][...], hi, preferred_element_type=F32)
            second = jnp.dot(mat[r][pl.ds(0, 2 * nb), :], lo, preferred_element_type=F32)
            both = first[: 2 * nb] + (first[2 * nb :] + second)
            for n, p in enumerate(cells):
                mine = both[:, n * ca : (n + 1) * ca]
                c = coef[r][pl.ds(p * cs, cs), :]
                c = jnp.concatenate([c] * fields, axis=0)
                new = (cell(psi[r][k], p) + mine[nb:]) + c * (cell(rhs[r], p) + mine[:nb])
                for f in range(fields):
                    psi[r][k + 1][f, pl.ds(p * cs, cs), :] = new[f * cs : (f + 1) * cs]

    loads[0].wait()
    pack_span(ROTOR, 0)
    pl.semaphore_wait(barrier, npass + nspan - 2)
    start_far(ROTOR, 0)
    for c in loads[1:3]:
        c.wait()
    start_far(STATOR, 0)
    start_near(ROTOR, 0)
    start_span(ROTOR, 0)
    start_near(STATOR, 0)
    pack_span(STATOR, 0)
    start_span(STATOR, 0)
    for o in range(1, npass):
        pl.semaphore_signal(
            gate, inc=1, device_id=(lax.rem(ip + o, npass), js), device_id_type=MESH
        )
    for c in loads[3:7]:
        c.wait()
    pack_face(0)
    pl.semaphore_wait(gate, npass - 1)
    start_face(0)

    for r in range(2):
        clear(r)
        build_matrix(r)
    for c in loads[7:]:
        c.wait()
    coef[ROTOR][...] = RELAX / coef[ROTOR][...]
    coef[STATOR][...] = RELAX / psi[STATOR][0][fields]
    interior(ROTOR, 0)
    interior(STATOR, 0)

    add_halos(ROTOR, 0, True)
    pack_face(1)
    start_face(1)
    add_halos(STATOR, 0, True)
    interior(ROTOR, 1)
    neighbour_inlets(add_inlet(0, False))
    interior(STATOR, 1)

    add_halos(ROTOR, 1, True)
    pack_face(2)
    start_face(2)
    add_halos(STATOR, 1, False)
    add_inlet(1, True)
    interior(ROTOR, 2)
    interior(STATOR, 2)

    for k in range(ITERS):
        for r in range(2):
            finish_sends(r, k)
        sent_faces(k).wait()
    add_halos(ROTOR, 2, False)
    add_inlet(2, False)
    add_halos(STATOR, 2, False)


def write_out(*refs):
    srcs, dsts, sem = refs[:2], refs[2:4], refs[4]
    copies = [pltpu.make_async_copy(srcs[n], dsts[n], sem.at[n]) for n in range(2)]
    for c in copies:
        c.start()
    for c in copies:
        c.wait()


def per_device(
    npass,
    nspan,
    psi_rotor,
    psi_stator,
    rhs_rotor,
    rhs_stator,
    kappa_rotor,
    kappa_stator,
    rotor_blocks,
    stator_blocks,
    interface_block,
    pass_counts,
    tile_source,
):
    fields, cp, cs, ca = psi_rotor.shape
    shape = (fields, cp * cs, ca)
    flat = [x.reshape(shape) for x in (psi_rotor, psi_stator, rhs_rotor, rhs_stator)]
    kaps = [x.reshape(cp * cs, ca) for x in (kappa_rotor, kappa_stator)]
    small = [x.transpose(1, 0, 2) for x in (rotor_blocks, stator_blocks)]
    small += [interface_block, tile_source]
    nb = fields * cs
    kx = 2 * nb + 16
    state = pltpu.VMEM(shape, F32)
    scratch = [state] * ITERS
    scratch += [pltpu.VMEM((fields + 1, cp * cs, ca), F32)]
    scratch += [state] * (ITERS - 1)
    scratch += [state] * 2
    scratch += [pltpu.VMEM((cp * cs, ca), F32)] * 2
    scratch += [pltpu.VMEM(((cp + 2) * nb, ca), BF16)] * 4
    scratch += [pltpu.VMEM((cp * kx, ca), BF16)] * 4
    scratch += [pltpu.VMEM((4 * nb, 5 * nb + 16), BF16)] * 2
    scratch += [pltpu.SMEM(x.shape, x.dtype) for x in small]
    scratch += [
        pltpu.VMEM((2, ITERS, 2, fields + 1, cs, ca), F32),
        pltpu.VMEM((2, fields, cs, ca), F32),
        pltpu.VMEM((2, ITERS, 2, fields + 1, cp, ca), F32),
        pltpu.VMEM((2, ITERS, 2, fields + 1, cp, ca), F32),
        pltpu.VMEM((ITERS, 1, ca), F32),
        pltpu.VMEM((2, fields, cs, ca), F32),
        pltpu.VMEM((2, fields, cp, ca), F32),
    ]
    scratch += [pltpu.VMEM((npass * nspan, 1, ca), F32)] * ITERS
    dma = pltpu.SemaphoreType.DMA
    scratch += [
        dma((10,)),
        dma((2, ITERS, 4)),
        dma((2, ITERS, 4)),
        dma((ITERS,)),
        dma((ITERS,)),
        pltpu.SemaphoreType.REGULAR,
    ]
    hbm = pl.BlockSpec(memory_space=pltpu.HBM)
    vmem = pl.BlockSpec(memory_space=pltpu.VMEM)
    done = pl.pallas_call(
        functools.partial(kernel, fields, cp, cs, ca, npass, nspan),
        out_shape=[pltpu.VMEM(shape, F32)] * 2,
        in_specs=[hbm] * 10 + [pl.BlockSpec(memory_space=pltpu.SMEM)],
        out_specs=[vmem] * 2,
        scratch_shapes=scratch,
        compiler_params=pltpu.CompilerParams(
            collective_id=0, has_side_effects=True, vmem_limit_bytes=32 * 1024 * 1024
        ),
    )(*[pltpu.with_memory_space_constraint(x, pltpu.HBM) for x in flat + kaps + small], pass_counts)
    out = pl.pallas_call(
        write_out,
        out_shape=[pltpu.HBM(shape, F32)] * 2,
        in_specs=[vmem] * 2,
        out_specs=[hbm] * 2,
        scratch_shapes=[dma((2,))],
    )(*[pltpu.with_memory_space_constraint(x, pltpu.VMEM) for x in done])
    return tuple(x.reshape(psi_rotor.shape) for x in out)


def solution(mesh):
    return jax.shard_map(
        functools.partial(per_device, mesh.shape["passage"], mesh.shape["span"]),
        mesh=mesh,
        in_specs=(
            P(None, "passage", "span", None),
            P(None, "passage", "span", None),
            P(None, "passage", "span", None),
            P(None, "passage", "span", None),
            P("passage", "span", None),
            P("passage", "span", None),
            P(),
            P(),
            P(),
            P("passage"),
            P(),
        ),
        out_specs=(P(None, "passage", "span", None), P(None, "passage", "span", None)),
        check_vma=False,
    )
```

```python
import functools

import jax
import jax.numpy as jnp
from jax import lax
from jax.experimental import pallas as pl
from jax.experimental.pallas import tpu as pltpu
from jax.sharding import PartitionSpec as P

ITERS = 3
RELAX = 0.8
MESH = pl.DeviceIdType.MESH
F32 = jnp.float32
BF16 = jnp.bfloat16
ROTOR, STATOR = 0, 1
SLOT = 16


def split(x):
    hi = x.astype(BF16)
    lo = (x - hi.astype(F32)).astype(BF16)
    return hi, lo


def kernel(fields, cp, cs, ca, npass, nspan, *refs):
    it = iter(refs)

    def take(n):
        return [next(it) for _ in range(n)]

    psi_in = take(2)
    rhs_in = take(2)
    kap_in = take(2)
    small_in = take(4)
    (counts,) = take(1)
    outs = take(2)
    psi = [take(ITERS) + [outs[r]] for r in range(2)]
    rhs = take(2)
    coef = take(2)
    cen = [take(2) for _ in range(2)]
    ext = [take(2) for _ in range(2)]
    mat = take(2)
    small = take(4)
    blocks, (iface, source) = small[:2], small[2:]
    (precv, psend, ssend, srecv, fsend, pcor, scor) = take(7)
    frecv = take(ITERS)
    (in_sem, hs_sem, hr_sem, fs_sem, fr_sem, gate) = take(6)

    nb = fields * cs
    kx = 2 * nb + 16
    plane = cp * cs
    others = npass * nspan - 1

    ip = lax.axis_index("passage")
    js = lax.axis_index("span")
    right = lax.rem(ip + 1, npass)
    left = lax.rem(ip + npass - 1, npass)
    has_next, has_prev = js < nspan - 1, js > 0

    def peer(o):
        return lax.rem(ip + o // nspan, npass), lax.rem(js + o % nspan, nspan)

    def each_peer(body):
        unroll = others if others < 64 else 1
        pl.loop(1, others + 1, unroll=unroll)(body)

    pairs = [
        (psi_in[0], psi[0][0]),
        (psi_in[1], psi[1][0].at[pl.ds(0, fields)]),
        (kap_in[1], psi[STATOR][0].at[fields]),
        *zip(small_in, small),
        (kap_in[0], coef[0]),
        (rhs_in[0], rhs[0]),
        (rhs_in[1], rhs[1]),
    ]
    loads = [pltpu.make_async_copy(a, b, in_sem.at[n]) for n, (a, b) in enumerate(pairs)]
    for c in loads:
        c.start()

    barrier = pltpu.get_barrier_semaphore()
    for o in range(1, npass):
        pl.semaphore_signal(
            barrier, inc=1, device_id=(lax.rem(ip + o, npass), js), device_id_type=MESH
        )
    for o in range(1, nspan):
        pl.semaphore_signal(
            barrier, inc=1, device_id=(ip, lax.rem(js + o, nspan)), device_id_type=MESH
        )

    for d, met in ((0, has_prev), (1, has_next)):

        @pl.when(jnp.logical_not(met))
        def _(d=d):
            for r in range(2):
                for k in range(ITERS):
                    srecv[r, k, d, pl.ds(0, fields)] = jnp.zeros((fields, cp, ca), F32)
                    srecv[r, k, d, fields] = jnp.ones((cp, ca), F32)

    def halo_copies(r, k):
        made = []
        n = fields + 1 if (r, k) == (STATOR, 0) else fields
        for d, p, target in ((0, cp - 1, (right, js)), (1, 0, (left, js))):
            made.append(
                pltpu.make_async_remote_copy(
                    src_ref=psend.at[d]
                    if (r, k) == (STATOR, 1)
                    else psi[r][k].at[:, pl.ds(p * cs, cs), :],
                    dst_ref=precv.at[r, k, d, pl.ds(0, n)],
                    send_sem=hs_sem.at[r, k, d],
                    recv_sem=hr_sem.at[r, k, d],
                    device_id=target,
                    device_id_type=MESH,
                )
            )
        for d, target in (
            (0, (ip, lax.rem(js + 1, nspan))),
            (1, (ip, lax.rem(js + nspan - 1, nspan))),
        ):
            made.append(
                pltpu.make_async_remote_copy(
                    src_ref=ssend.at[r, k, d, pl.ds(0, n)],
                    dst_ref=srecv.at[r, k, d, pl.ds(0, n)],
                    send_sem=hs_sem.at[r, k, 2 + d],
                    recv_sem=hr_sem.at[r, k, 2 + d],
                    device_id=target,
                    device_id_type=MESH,
                )
            )
        return made

    halos = {(r, k): halo_copies(r, k) for r in range(2) for k in range(ITERS)}

    def edge(s):
        return pl.ds(s, cp, stride=cs)

    def pack_span(r, k):
        for d, s in ((0, cs - 1), (1, 0)):
            for f in range(psi[r][k].shape[0]):
                ssend[r, k, d, f] = psi[r][k][f, edge(s), :]

    def start_pitch(r, k):
        to_right, to_left = halos[r, k][:2]

        @pl.when(ip == 0)
        def _():
            to_left.start()
            to_right.start()

        @pl.when(ip > 0)
        def _():
            to_right.start()
            to_left.start()

    def start_far(r, k):
        to_right, to_left = halos[r, k][:2]

        @pl.when(ip == 0)
        def _():
            to_left.start()

        @pl.when(ip > 0)
        def _():
            to_right.start()

    def start_near(r, k):
        to_right, to_left = halos[r, k][:2]

        @pl.when(ip == 0)
        def _():
            to_right.start()

        @pl.when(ip > 0)
        def _():
            to_left.start()

    def start_span(r, k):
        to_next, to_prev = halos[r, k][2:]

        @pl.when(has_next)
        def _():
            to_next.start()

        @pl.when(has_prev)
        def _():
            to_prev.start()

    def finish_sends(r, k):
        to_right, to_left, to_next, to_prev = halos[r, k]
        to_right.wait_send()
        to_left.wait_send()

        @pl.when(has_next)
        def _():
            to_next.wait_send()

        @pl.when(has_prev)
        def _():
            to_prev.wait_send()

    def mix(block, f, parts):
        acc = block(f, 0) * parts[0]
        for g in range(1, fields):
            acc = acc + block(f, g) * parts[g]
        return acc

    def span_terms(r, k):
        new = psi[r][k + 1]
        to_next, to_prev = halos[r, k][2:]

        @pl.when(has_prev)
        def _():
            to_next.wait_recv()

        @pl.when(has_next)
        def _():
            to_prev.wait_recv()

        for d, s in ((0, 0), (1, cs - 1)):
            c = coef[r][edge(s), :]
            parts = [srecv[r, k, d, g] for g in range(fields)]
            if (r, k) == (STATOR, 1):
                parts = [x + scor[d, g] for g, x in enumerate(parts)]
            for f in range(fields):
                acc = mix(lambda a, b: blocks[r][a, 3 + d, b], f, parts)
                new[f, edge(s), :] = new[f, edge(s), :] + c * acc

    def add_halos(r, k, send):
        span_terms(r, k)
        inner = face_sums(k + 1, range(1, cp - 1)) if send and r == ROTOR else None
        new = psi[r][k + 1]
        for d, p in ((0, 0), (1, cp - 1)):
            rows = pl.ds(p * cs, cs)
            c = coef[r][rows, :]
            halos[r, k][d].wait_recv()
            parts = [precv[r, k, d, g] for g in range(fields)]
            if (r, k) == (STATOR, 1):
                parts = [x + pcor[d, g] for g, x in enumerate(parts)]
            for f in range(fields):
                acc = mix(lambda a, b: blocks[r][a, 1 + d, b], f, parts)
                value = new[f, rows, :] + c * acc
                new[f, rows, :] = value
                if send and (r, k) == (STATOR, 0):
                    psend[1 - d, f] = value
            if send:
                halos[r, k + 1][1 - d].start()
        if send:
            pack_span(r, k + 1)
            start_span(r, k + 1)
        if inner is not None:
            pack_face(k + 1, inner)
            start_face(k + 1)

    lane = lax.broadcasted_iota(jnp.int32, (cs, ca), 1)
    at_slot = lane - SLOT * lax.broadcasted_iota(jnp.int32, (cs, ca), 0)
    wide = lax.broadcasted_iota(jnp.int32, (nb, ca), 1)

    def face_copy(k, o):
        return pltpu.make_async_remote_copy(
            src_ref=fsend.at[k],
            dst_ref=frecv[k].at[o],
            send_sem=fs_sem.at[k],
            recv_sem=fr_sem.at[k],
            device_id=peer(o),
            device_id_type=MESH,
        )

    def pick(x):
        return jnp.sum(x, axis=1, keepdims=True)

    def face_sums(k, where):
        weights = [jnp.where(p < counts[0], 1.0, 0.0).astype(F32) for p in where]
        sums = []
        for f in range(fields):
            parts = [
                w * psi[ROTOR][k][f, pl.ds(p * cs, cs), :] for w, p in zip(weights, where)
            ]
            while len(parts) > 1:
                parts = [sum(parts[n + 1 : n + 2], parts[n]) for n in range(0, len(parts), 2)]
            sums.append(parts[0])
        return sums

    def pack_face(k, inner):
        count = counts[0]
        ends = face_sums(k, (0, cp - 1))
        sums = [jnp.where(lane == ca - 1, a + b, 0.0) for a, b in zip(inner, ends)]
        tile = jnp.where(at_slot == fields, jnp.clip(count, 0, cp).astype(F32), 0.0)
        for f in range(fields):
            mixed = mix(lambda a, b: iface[a, b], f, sums)
            tile = jnp.where(at_slot == f, pick(mixed), tile)
        row = jnp.sum(tile, axis=0, keepdims=True)
        fsend[k] = row
        frecv[k][0] = row

    def start_face(k):
        each_peer(lambda o: face_copy(k, o).start())

    def all_faces(k):
        return pltpu.make_async_copy(
            frecv[k].at[pl.ds(1, others)], frecv[k].at[pl.ds(1, others)], fr_sem.at[k]
        )

    def sent_faces(k):
        return pltpu.make_async_copy(
            frecv[k].at[pl.ds(1, others)], frecv[k].at[pl.ds(1, others)], fs_sem.at[k]
        )

    def inlets(k, at):
        away = lax.rem(js - source[at] + nspan, nspan)
        total = frecv[k][away]
        for o in range(1, npass):
            total = total + frecv[k][o * nspan + away]
        total = jnp.broadcast_to(total, (cs, ca))
        count = pick(jnp.where(at_slot == fields, total, 0.0))
        made = []
        for f in range(fields):
            value = pick(jnp.where(at_slot == f, total, 0.0)) / count
            made.append(jnp.where(lane == 0, value, 0.0))
        return made

    def add_inlet(k, send):
        all_faces(k).wait()
        new = psi[STATOR][k + 1]
        values = inlets(k, js)

        def add(p):
            rows = pl.ds(p * cs, cs)
            for f in range(fields):
                new[f, rows, :] = new[f, rows, :] + coef[STATOR][rows, :] * values[f]

        add(0)
        add(cp - 1)
        if send:
            start_pitch(STATOR, k + 1)
        for p in range(1, cp - 1):
            add(p)
        if send:
            pack_span(STATOR, k + 1)
            start_span(STATOR, k + 1)
        return values

    def neighbour_inlets(own):
        for d in range(2):
            c = RELAX / precv[STATOR, 0, d, fields]
            for f in range(fields):
                pcor[d, f] = c * own[f]
        for d, s, at, met in (
            (0, cs - 1, jnp.maximum(js - 1, 0), has_prev),
            (1, 0, jnp.minimum(js + 1, nspan - 1), has_next),
        ):
            c = jnp.where(met, 1.0, 0.0) * (RELAX / srecv[STATOR, 0, d, fields])
            values = inlets(0, at)
            for f in range(fields):
                scor[d, f] = c * jnp.broadcast_to(values[f][s : s + 1], (cp, ca))

    def build_matrix(r):
        kk = 5 * nb + 16
        col = lax.broadcasted_iota(jnp.int32, (cs, kk), 1)
        row = lax.broadcasted_iota(jnp.int32, (cs, kk), 0)
        part = col // nb
        g_in = (col - part * nb) // cs
        s_in = col - part * nb - g_in * cs
        which = jnp.full((cs, kk), -1, jnp.int32)
        same = s_in == row
        which = jnp.where((part == 0) & same, 1, which)
        which = jnp.where((part == 2) & same, 2, which)
        which = jnp.where((part == 3) & same, 5, which)
        which = jnp.where((part == 4) & same, 6, which)
        which = jnp.where((part == 1) & (s_in + 1 == row), 3, which)
        which = jnp.where((part == 1) & (s_in == row + 1), 4, which)
        code = jnp.where(which >= 0, which * 8 + g_in, -1)
        middle = jnp.where((part == 1) & same, g_in, -1)
        near, main = [], []
        masks = [[code == (b * 8 + g) for g in range(fields)] for b in range(1, 7)]
        centre = [middle == g for g in range(fields)]
        for f in range(fields):
            acc = jnp.zeros((cs, kk), F32)
            mid = jnp.zeros((cs, kk), F32)
            for g in range(fields):
                mid = jnp.where(centre[g], -RELAX * blocks[r][f, 0, g], mid)
                for b in range(1, 7):
                    acc = jnp.where(masks[b - 1][g], blocks[r][f, b, g], acc)
            near.append(acc)
            main.append(mid)
        hi, lo = split(jnp.concatenate(near + main, axis=0))
        mat[r][pl.ds(0, 2 * nb), :] = hi
        mat[r][pl.ds(2 * nb, 2 * nb), :] = lo

    def clear(r):
        for n in range(2):
            cen[r][n][pl.ds(0, nb), :] = jnp.zeros((nb, ca), BF16)
            cen[r][n][pl.ds((cp + 1) * nb, nb), :] = jnp.zeros((nb, ca), BF16)
            for p in range(cp):
                ext[r][n][pl.ds(p * kx + 2 * nb, 16), :] = jnp.zeros((16, ca), BF16)

    def cell(ref, p):
        return jnp.concatenate([ref[f, pl.ds(p * cs, cs), :] for f in range(fields)], axis=0)

    def store_split(r, k, p):
        new = cell(psi[r][k], p)
        before = jnp.where(wide == 0, 0.0, pltpu.roll(new, 1, 1))
        after = jnp.where(wide == ca - 1, 0.0, pltpu.roll(new, ca - 1, 1))
        for buf, at, value in (
            (cen, (p + 1) * nb, new),
            (ext, p * kx, before),
            (ext, p * kx + nb, after),
        ):
            hi, lo = split(value)
            buf[r][0][pl.ds(at, nb), :] = hi
            buf[r][1][pl.ds(at, nb), :] = lo

    def columns(r, n, p):
        return jnp.concatenate(
            [cen[r][n][pl.ds(p * nb, 3 * nb), :], ext[r][n][pl.ds(p * kx, kx), :]], axis=0
        )

    def interior(r, k):
        for p in range(cp):
            store_split(r, k, p)
        for q in range(cp // 2):
            cells = (2 * q, 2 * q + 1)
            hi = jnp.concatenate([columns(r, 0, p) for p in cells], axis=1)
            lo = jnp.concatenate([columns(r, 1, p) for p in cells], axis=1)
            first = jnp.dot(mat[r][...], hi, preferred_element_type=F32)
            second = jnp.dot(mat[r][pl.ds(0, 2 * nb), :], lo, preferred_element_type=F32)
            both = first[: 2 * nb] + (first[2 * nb :] + second)
            for n, p in enumerate(cells):
                mine = both[:, n * ca : (n + 1) * ca]
                c = coef[r][pl.ds(p * cs, cs), :]
                c = jnp.concatenate([c] * fields, axis=0)
                new = (cell(psi[r][k], p) + mine[nb:]) + c * (cell(rhs[r], p) + mine[:nb])
                for f in range(fields):
                    psi[r][k + 1][f, pl.ds(p * cs, cs), :] = new[f * cs : (f + 1) * cs]

    loads[0].wait()
    pack_span(ROTOR, 0)
    pl.semaphore_wait(barrier, npass + nspan - 2)
    start_far(ROTOR, 0)
    for c in loads[1:3]:
        c.wait()
    start_far(STATOR, 0)
    start_near(ROTOR, 0)
    start_span(ROTOR, 0)
    start_near(STATOR, 0)
    pack_span(STATOR, 0)
    start_span(STATOR, 0)
    for o in range(1, npass):
        pl.semaphore_signal(
            gate, inc=1, device_id=(lax.rem(ip + o, npass), js), device_id_type=MESH
        )
    for c in loads[3:7]:
        c.wait()
    pack_face(0, face_sums(0, range(1, cp - 1)))
    pl.semaphore_wait(gate, npass - 1)
    start_face(0)

    for r in range(2):
        clear(r)
        build_matrix(r)
    for c in loads[7:]:
        c.wait()
    coef[ROTOR][...] = RELAX / coef[ROTOR][...]
    coef[STATOR][...] = RELAX / psi[STATOR][0][fields]
    interior(ROTOR, 0)
    interior(STATOR, 0)

    add_halos(ROTOR, 0, True)
    add_halos(STATOR, 0, True)
    interior(ROTOR, 1)
    neighbour_inlets(add_inlet(0, False))
    interior(STATOR, 1)

    add_halos(ROTOR, 1, True)
    add_halos(STATOR, 1, False)
    add_inlet(1, True)
    interior(ROTOR, 2)
    interior(STATOR, 2)

    for k in range(ITERS):
        for r in range(2):
            finish_sends(r, k)
        sent_faces(k).wait()
    add_halos(ROTOR, 2, False)
    add_inlet(2, False)
    add_halos(STATOR, 2, False)


def write_out(*refs):
    srcs, dsts, sem = refs[:2], refs[2:4], refs[4]
    copies = [pltpu.make_async_copy(srcs[n], dsts[n], sem.at[n]) for n in range(2)]
    for c in copies:
        c.start()
    for c in copies:
        c.wait()


def per_device(
    npass,
    nspan,
    psi_rotor,
    psi_stator,
    rhs_rotor,
    rhs_stator,
    kappa_rotor,
    kappa_stator,
    rotor_blocks,
    stator_blocks,
    interface_block,
    pass_counts,
    tile_source,
):
    fields, cp, cs, ca = psi_rotor.shape
    shape = (fields, cp * cs, ca)
    flat = [x.reshape(shape) for x in (psi_rotor, psi_stator, rhs_rotor, rhs_stator)]
    kaps = [x.reshape(cp * cs, ca) for x in (kappa_rotor, kappa_stator)]
    small = [x.transpose(1, 0, 2) for x in (rotor_blocks, stator_blocks)]
    small += [interface_block, tile_source]
    nb = fields * cs
    kx = 2 * nb + 16
    state = pltpu.VMEM(shape, F32)
    scratch = [state] * ITERS
    scratch += [pltpu.VMEM((fields + 1, cp * cs, ca), F32)]
    scratch += [state] * (ITERS - 1)
    scratch += [state] * 2
    scratch += [pltpu.VMEM((cp * cs, ca), F32)] * 2
    scratch += [pltpu.VMEM(((cp + 2) * nb, ca), BF16)] * 4
    scratch += [pltpu.VMEM((cp * kx, ca), BF16)] * 4
    scratch += [pltpu.VMEM((4 * nb, 5 * nb + 16), BF16)] * 2
    scratch += [pltpu.SMEM(x.shape, x.dtype) for x in small]
    scratch += [
        pltpu.VMEM((2, ITERS, 2, fields + 1, cs, ca), F32),
        pltpu.VMEM((2, fields, cs, ca), F32),
        pltpu.VMEM((2, ITERS, 2, fields + 1, cp, ca), F32),
        pltpu.VMEM((2, ITERS, 2, fields + 1, cp, ca), F32),
        pltpu.VMEM((ITERS, 1, ca), F32),
        pltpu.VMEM((2, fields, cs, ca), F32),
        pltpu.VMEM((2, fields, cp, ca), F32),
    ]
    scratch += [pltpu.VMEM((npass * nspan, 1, ca), F32)] * ITERS
    dma = pltpu.SemaphoreType.DMA
    scratch += [
        dma((10,)),
        dma((2, ITERS, 4)),
        dma((2, ITERS, 4)),
        dma((ITERS,)),
        dma((ITERS,)),
        pltpu.SemaphoreType.REGULAR,
    ]
    hbm = pl.BlockSpec(memory_space=pltpu.HBM)
    vmem = pl.BlockSpec(memory_space=pltpu.VMEM)
    done = pl.pallas_call(
        functools.partial(kernel, fields, cp, cs, ca, npass, nspan),
        out_shape=[pltpu.VMEM(shape, F32)] * 2,
        in_specs=[hbm] * 10 + [pl.BlockSpec(memory_space=pltpu.SMEM)],
        out_specs=[vmem] * 2,
        scratch_shapes=scratch,
        compiler_params=pltpu.CompilerParams(
            collective_id=0, has_side_effects=True, vmem_limit_bytes=32 * 1024 * 1024
        ),
    )(*[pltpu.with_memory_space_constraint(x, pltpu.HBM) for x in flat + kaps + small], pass_counts)
    out = pl.pallas_call(
        write_out,
        out_shape=[pltpu.HBM(shape, F32)] * 2,
        in_specs=[vmem] * 2,
        out_specs=[hbm] * 2,
        scratch_shapes=[dma((2,))],
    )(*[pltpu.with_memory_space_constraint(x, pltpu.VMEM) for x in done])
    return tuple(x.reshape(psi_rotor.shape) for x in out)


def solution(mesh):
    return jax.shard_map(
        functools.partial(per_device, mesh.shape["passage"], mesh.shape["span"]),
        mesh=mesh,
        in_specs=(
            P(None, "passage", "span", None),
            P(None, "passage", "span", None),
            P(None, "passage", "span", None),
            P(None, "passage", "span", None),
            P("passage", "span", None),
            P("passage", "span", None),
            P(),
            P(),
            P(),
            P("passage"),
            P(),
        ),
        out_specs=(P(None, "passage", "span", None), P(None, "passage", "span", None)),
        check_vma=False,
    )
```

```python
import functools

import jax
import jax.numpy as jnp
from jax import lax
from jax.experimental import pallas as pl
from jax.experimental.pallas import tpu as pltpu
from jax.sharding import PartitionSpec as P

ITERS = 3
RELAX = 0.8
MESH = pl.DeviceIdType.MESH
F32 = jnp.float32
BF16 = jnp.bfloat16
ROTOR, STATOR = 0, 1
SLOT = 16


def split(x):
    hi = x.astype(BF16)
    lo = (x - hi.astype(F32)).astype(BF16)
    return hi, lo


def kernel(fields, cp, cs, ca, npass, nspan, *refs):
    it = iter(refs)

    def take(n):
        return [next(it) for _ in range(n)]

    psi_in = take(2)
    rhs_in = take(2)
    kap_in = take(2)
    small_in = take(4)
    (counts,) = take(1)
    outs = take(2)
    psi = [take(ITERS) + [outs[r]] for r in range(2)]
    rhs = take(2)
    coef = take(2)
    cen = [take(2) for _ in range(2)]
    ext = [take(2) for _ in range(2)]
    mat = take(2)
    small = take(4)
    blocks, (iface, source) = small[:2], small[2:]
    (precv, psend, ssend, srecv, fsend, pcor, scor) = take(7)
    frecv = take(ITERS)
    (in_sem, hs_sem, hr_sem, fs_sem, fr_sem, gate) = take(6)

    nb = fields * cs
    kx = 2 * nb + 16
    plane = cp * cs
    others = npass * nspan - 1

    ip = lax.axis_index("passage")
    js = lax.axis_index("span")
    right = lax.rem(ip + 1, npass)
    left = lax.rem(ip + npass - 1, npass)
    has_next, has_prev = js < nspan - 1, js > 0

    def peer(o):
        return lax.rem(ip + o // nspan, npass), lax.rem(js + o % nspan, nspan)

    def each_peer(body):
        unroll = others if others < 64 else 1
        pl.loop(1, others + 1, unroll=unroll)(body)

    pairs = [
        (psi_in[0], psi[0][0]),
        (psi_in[1], psi[1][0].at[pl.ds(0, fields)]),
        (kap_in[1], psi[STATOR][0].at[fields]),
        *zip(small_in, small),
        (kap_in[0], coef[0]),
        (rhs_in[0], rhs[0]),
        (rhs_in[1], rhs[1]),
    ]
    loads = [pltpu.make_async_copy(a, b, in_sem.at[n]) for n, (a, b) in enumerate(pairs)]
    for c in loads:
        c.start()

    barrier = pltpu.get_barrier_semaphore()
    for o in range(1, npass):
        pl.semaphore_signal(
            barrier, inc=1, device_id=(lax.rem(ip + o, npass), js), device_id_type=MESH
        )
    for o in range(1, nspan):
        pl.semaphore_signal(
            barrier, inc=1, device_id=(ip, lax.rem(js + o, nspan)), device_id_type=MESH
        )

    for d, met in ((0, has_prev), (1, has_next)):

        @pl.when(jnp.logical_not(met))
        def _(d=d):
            for r in range(2):
                for k in range(ITERS):
                    srecv[r, k, d, pl.ds(0, fields)] = jnp.zeros((fields, cp, ca), F32)
                    srecv[r, k, d, fields] = jnp.ones((cp, ca), F32)

    def halo_copies(r, k):
        made = []
        n = fields + 1 if (r, k) == (STATOR, 0) else fields
        for d, p, target in ((0, cp - 1, (right, js)), (1, 0, (left, js))):
            made.append(
                pltpu.make_async_remote_copy(
                    src_ref=psend.at[d]
                    if (r, k) == (STATOR, 1)
                    else psi[r][k].at[:, pl.ds(p * cs, cs), :],
                    dst_ref=precv.at[r, k, d, pl.ds(0, n)],
                    send_sem=hs_sem.at[r, k, d],
                    recv_sem=hr_sem.at[r, k, d],
                    device_id=target,
                    device_id_type=MESH,
                )
            )
        for d, target in (
            (0, (ip, lax.rem(js + 1, nspan))),
            (1, (ip, lax.rem(js + nspan - 1, nspan))),
        ):
            made.append(
                pltpu.make_async_remote_copy(
                    src_ref=ssend.at[r, k, d, pl.ds(0, n)],
                    dst_ref=srecv.at[r, k, d, pl.ds(0, n)],
                    send_sem=hs_sem.at[r, k, 2 + d],
                    recv_sem=hr_sem.at[r, k, 2 + d],
                    device_id=target,
                    device_id_type=MESH,
                )
            )
        return made

    halos = {(r, k): halo_copies(r, k) for r in range(2) for k in range(ITERS)}

    def edge(s):
        return pl.ds(s, cp, stride=cs)

    def pack_span(r, k):
        for d, s in ((0, cs - 1), (1, 0)):
            for f in range(psi[r][k].shape[0]):
                ssend[r, k, d, f] = psi[r][k][f, edge(s), :]

    def start_pitch(r, k):
        to_right, to_left = halos[r, k][:2]

        @pl.when(ip == 0)
        def _():
            to_left.start()
            to_right.start()

        @pl.when(ip > 0)
        def _():
            to_right.start()
            to_left.start()

    def start_far(r, k):
        to_right, to_left = halos[r, k][:2]

        @pl.when(ip == 0)
        def _():
            to_left.start()

        @pl.when(ip > 0)
        def _():
            to_right.start()

    def start_near(r, k):
        to_right, to_left = halos[r, k][:2]

        @pl.when(ip == 0)
        def _():
            to_right.start()

        @pl.when(ip > 0)
        def _():
            to_left.start()

    def start_span(r, k):
        to_next, to_prev = halos[r, k][2:]

        @pl.when(has_next)
        def _():
            to_next.start()

        @pl.when(has_prev)
        def _():
            to_prev.start()

    def finish_sends(r, k):
        to_right, to_left, to_next, to_prev = halos[r, k]
        to_right.wait_send()
        to_left.wait_send()

        @pl.when(has_next)
        def _():
            to_next.wait_send()

        @pl.when(has_prev)
        def _():
            to_prev.wait_send()

    def mix(block, f, parts):
        acc = block(f, 0) * parts[0]
        for g in range(1, fields):
            acc = acc + block(f, g) * parts[g]
        return acc

    def span_terms(r, k):
        new = psi[r][k + 1]
        to_next, to_prev = halos[r, k][2:]

        @pl.when(has_prev)
        def _():
            to_next.wait_recv()

        @pl.when(has_next)
        def _():
            to_prev.wait_recv()

        for d, s in ((0, 0), (1, cs - 1)):
            c = coef[r][edge(s), :]
            parts = [srecv[r, k, d, g] for g in range(fields)]
            if (r, k) == (STATOR, 1):
                parts = [x + scor[d, g] for g, x in enumerate(parts)]
            for f in range(fields):
                acc = mix(lambda a, b: blocks[r][a, 3 + d, b], f, parts)
                new[f, edge(s), :] = new[f, edge(s), :] + c * acc

    def add_halos(r, k, send):
        span_terms(r, k)
        inner = face_sums(k + 1, range(1, cp - 1)) if send and r == ROTOR else None
        new = psi[r][k + 1]
        for d, p in ((0, 0), (1, cp - 1)):
            rows = pl.ds(p * cs, cs)
            c = coef[r][rows, :]
            halos[r, k][d].wait_recv()
            parts = [precv[r, k, d, g] for g in range(fields)]
            if (r, k) == (STATOR, 1):
                parts = [x + pcor[d, g] for g, x in enumerate(parts)]
            for f in range(fields):
                acc = mix(lambda a, b: blocks[r][a, 1 + d, b], f, parts)
                value = new[f, rows, :] + c * acc
                new[f, rows, :] = value
                if send and (r, k) == (STATOR, 0):
                    psend[1 - d, f] = value
            if send:
                halos[r, k + 1][1 - d].start()
        if send:
            pack_span(r, k + 1)
            start_span(r, k + 1)
        if inner is not None:
            pack_face(k + 1, inner)
            start_face(k + 1)

    lane = lax.broadcasted_iota(jnp.int32, (cs, ca), 1)
    at_slot = lane - SLOT * lax.broadcasted_iota(jnp.int32, (cs, ca), 0)
    wide = lax.broadcasted_iota(jnp.int32, (nb, ca), 1)

    def face_copy(k, o):
        return pltpu.make_async_remote_copy(
            src_ref=fsend.at[k],
            dst_ref=frecv[k].at[o],
            send_sem=fs_sem.at[k],
            recv_sem=fr_sem.at[k],
            device_id=peer(o),
            device_id_type=MESH,
        )

    def pick(x):
        return jnp.sum(x, axis=1, keepdims=True)

    def face_sums(k, where):
        weights = [jnp.where(p < counts[0], 1.0, 0.0).astype(F32) for p in where]
        sums = []
        for f in range(fields):
            parts = [
                w * psi[ROTOR][k][f, pl.ds(p * cs, cs), :] for w, p in zip(weights, where)
            ]
            while len(parts) > 1:
                parts = [sum(parts[n + 1 : n + 2], parts[n]) for n in range(0, len(parts), 2)]
            sums.append(parts[0])
        return sums

    def pack_face(k, inner):
        count = counts[0]
        ends = face_sums(k, (0, cp - 1))
        sums = [jnp.where(lane == ca - 1, a + b, 0.0) for a, b in zip(inner, ends)]
        tile = jnp.where(at_slot == fields, jnp.clip(count, 0, cp).astype(F32), 0.0)
        for f in range(fields):
            mixed = mix(lambda a, b: iface[a, b], f, sums)
            tile = jnp.where(at_slot == f, pick(mixed), tile)
        row = jnp.sum(tile, axis=0, keepdims=True)
        fsend[k] = row
        frecv[k][0] = row

    def start_face(k):
        each_peer(lambda o: face_copy(k, o).start())

    def all_faces(k):
        return pltpu.make_async_copy(
            frecv[k].at[pl.ds(1, others)], frecv[k].at[pl.ds(1, others)], fr_sem.at[k]
        )

    def sent_faces(k):
        return pltpu.make_async_copy(
            frecv[k].at[pl.ds(1, others)], frecv[k].at[pl.ds(1, others)], fs_sem.at[k]
        )

    def inlets(k, at):
        away = lax.rem(js - source[at] + nspan, nspan)
        total = frecv[k][away]
        for o in range(1, npass):
            total = total + frecv[k][o * nspan + away]
        total = jnp.broadcast_to(total, (cs, ca))
        count = pick(jnp.where(at_slot == fields, total, 0.0))
        made = []
        for f in range(fields):
            value = pick(jnp.where(at_slot == f, total, 0.0)) / count
            made.append(jnp.where(lane == 0, value, 0.0))
        return made

    def add_inlet(k, send):
        all_faces(k).wait()
        new = psi[STATOR][k + 1]
        values = inlets(k, js)

        def add(p):
            rows = pl.ds(p * cs, cs)
            for f in range(fields):
                new[f, rows, :] = new[f, rows, :] + coef[STATOR][rows, :] * values[f]

        add(0)
        add(cp - 1)
        if send:
            start_pitch(STATOR, k + 1)
        for p in range(1, cp - 1):
            add(p)
        if send:
            pack_span(STATOR, k + 1)
            start_span(STATOR, k + 1)
        return values

    def neighbour_inlets(own):
        for d in range(2):
            c = RELAX / precv[STATOR, 0, d, fields]
            for f in range(fields):
                pcor[d, f] = c * own[f]
        for d, s, at, met in (
            (0, cs - 1, jnp.maximum(js - 1, 0), has_prev),
            (1, 0, jnp.minimum(js + 1, nspan - 1), has_next),
        ):
            c = jnp.where(met, 1.0, 0.0) * (RELAX / srecv[STATOR, 0, d, fields])
            values = inlets(0, at)
            for f in range(fields):
                scor[d, f] = c * jnp.broadcast_to(values[f][s : s + 1], (cp, ca))

    def build_matrix(r):
        kk = 5 * nb + 16
        col = lax.broadcasted_iota(jnp.int32, (cs, kk), 1)
        row = lax.broadcasted_iota(jnp.int32, (cs, kk), 0)
        part = col // nb
        g_in = (col - part * nb) // cs
        s_in = col - part * nb - g_in * cs
        which = jnp.full((cs, kk), -1, jnp.int32)
        same = s_in == row
        which = jnp.where((part == 0) & same, 1, which)
        which = jnp.where((part == 2) & same, 2, which)
        which = jnp.where((part == 3) & same, 5, which)
        which = jnp.where((part == 4) & same, 6, which)
        which = jnp.where((part == 1) & (s_in + 1 == row), 3, which)
        which = jnp.where((part == 1) & (s_in == row + 1), 4, which)
        code = jnp.where(which >= 0, which * 8 + g_in, -1)
        middle = jnp.where((part == 1) & same, g_in, -1)
        near, main = [], []
        masks = [[code == (b * 8 + g) for g in range(fields)] for b in range(1, 7)]
        centre = [middle == g for g in range(fields)]
        for f in range(fields):
            acc = jnp.zeros((cs, kk), F32)
            mid = jnp.zeros((cs, kk), F32)
            for g in range(fields):
                mid = jnp.where(centre[g], -RELAX * blocks[r][f, 0, g], mid)
                for b in range(1, 7):
                    acc = jnp.where(masks[b - 1][g], blocks[r][f, b, g], acc)
            near.append(acc)
            main.append(mid)
        hi, lo = split(jnp.concatenate(near + main, axis=0))
        mat[r][pl.ds(0, 2 * nb), :] = hi
        mat[r][pl.ds(2 * nb, 2 * nb), :] = lo

    def clear(r):
        for n in range(2):
            cen[r][n][pl.ds(0, nb), :] = jnp.zeros((nb, ca), BF16)
            cen[r][n][pl.ds((cp + 1) * nb, nb), :] = jnp.zeros((nb, ca), BF16)
            for p in range(cp):
                ext[r][n][pl.ds(p * kx + 2 * nb, 16), :] = jnp.zeros((16, ca), BF16)

    def cell(ref, p):
        return jnp.concatenate([ref[f, pl.ds(p * cs, cs), :] for f in range(fields)], axis=0)

    def store_split(r, k, p):
        new = cell(psi[r][k], p)
        before = jnp.where(wide == 0, 0.0, pltpu.roll(new, 1, 1))
        after = jnp.where(wide == ca - 1, 0.0, pltpu.roll(new, ca - 1, 1))
        for buf, at, value in (
            (cen, (p + 1) * nb, new),
            (ext, p * kx, before),
            (ext, p * kx + nb, after),
        ):
            hi, lo = split(value)
            buf[r][0][pl.ds(at, nb), :] = hi
            buf[r][1][pl.ds(at, nb), :] = lo

    def columns(r, n, p):
        return jnp.concatenate(
            [cen[r][n][pl.ds(p * nb, 3 * nb), :], ext[r][n][pl.ds(p * kx, kx), :]], axis=0
        )

    def interior(r, k):
        for p in range(cp):
            store_split(r, k, p)
        for q in range(cp // 2):
            cells = (2 * q, 2 * q + 1)
            hi = jnp.concatenate([columns(r, 0, p) for p in cells], axis=1)
            lo = jnp.concatenate([columns(r, 1, p) for p in cells], axis=1)
            first = jnp.dot(mat[r][...], hi, preferred_element_type=F32)
            second = jnp.dot(mat[r][pl.ds(0, 2 * nb), :], lo, preferred_element_type=F32)
            both = first[: 2 * nb] + (first[2 * nb :] + second)
            for n, p in enumerate(cells):
                mine = both[:, n * ca : (n + 1) * ca]
                c = coef[r][pl.ds(p * cs, cs), :]
                c = jnp.concatenate([c] * fields, axis=0)
                new = (cell(psi[r][k], p) + mine[nb:]) + c * (cell(rhs[r], p) + mine[:nb])
                for f in range(fields):
                    psi[r][k + 1][f, pl.ds(p * cs, cs), :] = new[f * cs : (f + 1) * cs]

    loads[0].wait()
    pack_span(ROTOR, 0)
    pl.semaphore_wait(barrier, npass + nspan - 2)
    start_far(ROTOR, 0)
    for o in range(1, npass):
        pl.semaphore_signal(
            gate, inc=1, device_id=(lax.rem(ip + o, npass), js), device_id_type=MESH
        )
    for c in loads[1:3]:
        c.wait()
    start_far(STATOR, 0)
    start_near(ROTOR, 0)
    start_span(ROTOR, 0)
    start_near(STATOR, 0)
    pack_span(STATOR, 0)
    start_span(STATOR, 0)
    for c in loads[3:7]:
        c.wait()
    pack_face(0, face_sums(0, range(1, cp - 1)))

    for r in range(2):
        clear(r)
        build_matrix(r)
    for c in loads[7:]:
        c.wait()
    coef[ROTOR][...] = RELAX / coef[ROTOR][...]
    coef[STATOR][...] = RELAX / psi[STATOR][0][fields]
    interior(ROTOR, 0)
    interior(STATOR, 0)
    pl.semaphore_wait(gate, npass - 1)
    start_face(0)

    add_halos(ROTOR, 0, True)
    add_halos(STATOR, 0, True)
    interior(ROTOR, 1)
    neighbour_inlets(add_inlet(0, False))
    interior(STATOR, 1)

    add_halos(ROTOR, 1, True)
    add_halos(STATOR, 1, False)
    add_inlet(1, True)
    interior(ROTOR, 2)
    interior(STATOR, 2)

    for k in range(ITERS):
        for r in range(2):
            finish_sends(r, k)
        sent_faces(k).wait()
    add_halos(ROTOR, 2, False)
    add_inlet(2, False)
    add_halos(STATOR, 2, False)


def write_out(*refs):
    srcs, dsts, sem = refs[:2], refs[2:4], refs[4]
    copies = [pltpu.make_async_copy(srcs[n], dsts[n], sem.at[n]) for n in range(2)]
    for c in copies:
        c.start()
    for c in copies:
        c.wait()


def per_device(
    npass,
    nspan,
    psi_rotor,
    psi_stator,
    rhs_rotor,
    rhs_stator,
    kappa_rotor,
    kappa_stator,
    rotor_blocks,
    stator_blocks,
    interface_block,
    pass_counts,
    tile_source,
):
    fields, cp, cs, ca = psi_rotor.shape
    shape = (fields, cp * cs, ca)
    flat = [x.reshape(shape) for x in (psi_rotor, psi_stator, rhs_rotor, rhs_stator)]
    kaps = [x.reshape(cp * cs, ca) for x in (kappa_rotor, kappa_stator)]
    small = [x.transpose(1, 0, 2) for x in (rotor_blocks, stator_blocks)]
    small += [interface_block, tile_source]
    nb = fields * cs
    kx = 2 * nb + 16
    state = pltpu.VMEM(shape, F32)
    scratch = [state] * ITERS
    scratch += [pltpu.VMEM((fields + 1, cp * cs, ca), F32)]
    scratch += [state] * (ITERS - 1)
    scratch += [state] * 2
    scratch += [pltpu.VMEM((cp * cs, ca), F32)] * 2
    scratch += [pltpu.VMEM(((cp + 2) * nb, ca), BF16)] * 4
    scratch += [pltpu.VMEM((cp * kx, ca), BF16)] * 4
    scratch += [pltpu.VMEM((4 * nb, 5 * nb + 16), BF16)] * 2
    scratch += [pltpu.SMEM(x.shape, x.dtype) for x in small]
    scratch += [
        pltpu.VMEM((2, ITERS, 2, fields + 1, cs, ca), F32),
        pltpu.VMEM((2, fields, cs, ca), F32),
        pltpu.VMEM((2, ITERS, 2, fields + 1, cp, ca), F32),
        pltpu.VMEM((2, ITERS, 2, fields + 1, cp, ca), F32),
        pltpu.VMEM((ITERS, 1, ca), F32),
        pltpu.VMEM((2, fields, cs, ca), F32),
        pltpu.VMEM((2, fields, cp, ca), F32),
    ]
    scratch += [pltpu.VMEM((npass * nspan, 1, ca), F32)] * ITERS
    dma = pltpu.SemaphoreType.DMA
    scratch += [
        dma((10,)),
        dma((2, ITERS, 4)),
        dma((2, ITERS, 4)),
        dma((ITERS,)),
        dma((ITERS,)),
        pltpu.SemaphoreType.REGULAR,
    ]
    hbm = pl.BlockSpec(memory_space=pltpu.HBM)
    vmem = pl.BlockSpec(memory_space=pltpu.VMEM)
    done = pl.pallas_call(
        functools.partial(kernel, fields, cp, cs, ca, npass, nspan),
        out_shape=[pltpu.VMEM(shape, F32)] * 2,
        in_specs=[hbm] * 10 + [pl.BlockSpec(memory_space=pltpu.SMEM)],
        out_specs=[vmem] * 2,
        scratch_shapes=scratch,
        compiler_params=pltpu.CompilerParams(
            collective_id=0, has_side_effects=True, vmem_limit_bytes=32 * 1024 * 1024
        ),
    )(*[pltpu.with_memory_space_constraint(x, pltpu.HBM) for x in flat + kaps + small], pass_counts)
    out = pl.pallas_call(
        write_out,
        out_shape=[pltpu.HBM(shape, F32)] * 2,
        in_specs=[vmem] * 2,
        out_specs=[hbm] * 2,
        scratch_shapes=[dma((2,))],
    )(*[pltpu.with_memory_space_constraint(x, pltpu.VMEM) for x in done])
    return tuple(x.reshape(psi_rotor.shape) for x in out)


def solution(mesh):
    return jax.shard_map(
        functools.partial(per_device, mesh.shape["passage"], mesh.shape["span"]),
        mesh=mesh,
        in_specs=(
            P(None, "passage", "span", None),
            P(None, "passage", "span", None),
            P(None, "passage", "span", None),
            P(None, "passage", "span", None),
            P("passage", "span", None),
            P("passage", "span", None),
            P(),
            P(),
            P(),
            P("passage"),
            P(),
        ),
        out_specs=(P(None, "passage", "span", None), P(None, "passage", "span", None)),
        check_vma=False,
    )
```

```python
import functools

import jax
import jax.numpy as jnp
from jax import lax
from jax.experimental import pallas as pl
from jax.experimental.pallas import tpu as pltpu
from jax.sharding import PartitionSpec as P

ITERS = 3
RELAX = 0.8
MESH = pl.DeviceIdType.MESH
F32 = jnp.float32
BF16 = jnp.bfloat16
ROTOR, STATOR = 0, 1
SLOT = 16


def split(x):
    hi = x.astype(BF16)
    lo = (x - hi.astype(F32)).astype(BF16)
    return hi, lo


def kernel(fields, cp, cs, ca, npass, nspan, *refs):
    it = iter(refs)

    def take(n):
        return [next(it) for _ in range(n)]

    psi_in = take(2)
    rhs_in = take(2)
    kap_in = take(2)
    small_in = take(4)
    (counts,) = take(1)
    outs = take(2)
    psi = [take(ITERS) + [outs[r]] for r in range(2)]
    rhs = take(2)
    coef = take(2)
    cen = [take(2) for _ in range(2)]
    ext = [take(2) for _ in range(2)]
    mat = take(2)
    small = take(4)
    blocks, (iface, source) = small[:2], small[2:]
    (precv, psend, ssend, srecv, fsend, pcor, scor) = take(7)
    frecv = take(ITERS)
    (in_sem, hs_sem, hr_sem, fs_sem, fr_sem, gate) = take(6)

    nb = fields * cs
    kx = 2 * nb + 16
    plane = cp * cs
    others = npass * nspan - 1

    ip = lax.axis_index("passage")
    js = lax.axis_index("span")
    right = lax.rem(ip + 1, npass)
    left = lax.rem(ip + npass - 1, npass)
    has_next, has_prev = js < nspan - 1, js > 0

    def peer(o):
        return lax.rem(ip + o // nspan, npass), lax.rem(js + o % nspan, nspan)

    def each_peer(body):
        unroll = others if others < 64 else 1
        pl.loop(1, others + 1, unroll=unroll)(body)

    pairs = [
        (psi_in[0], psi[0][0]),
        (psi_in[1], psi[1][0].at[pl.ds(0, fields)]),
        (kap_in[1], psi[STATOR][0].at[fields]),
        *zip(small_in, small),
        (kap_in[0], coef[0]),
        (rhs_in[0], rhs[0]),
        (rhs_in[1], rhs[1]),
    ]
    loads = [pltpu.make_async_copy(a, b, in_sem.at[n]) for n, (a, b) in enumerate(pairs)]
    for c in loads:
        c.start()

    barrier = pltpu.get_barrier_semaphore()
    for o in range(1, npass):
        pl.semaphore_signal(
            barrier, inc=1, device_id=(lax.rem(ip + o, npass), js), device_id_type=MESH
        )
    for o in range(1, nspan):
        pl.semaphore_signal(
            barrier, inc=1, device_id=(ip, lax.rem(js + o, nspan)), device_id_type=MESH
        )

    for d, met in ((0, has_prev), (1, has_next)):

        @pl.when(jnp.logical_not(met))
        def _(d=d):
            for r in range(2):
                for k in range(ITERS):
                    srecv[r, k, d, pl.ds(0, fields)] = jnp.zeros((fields, cp, ca), F32)
                    srecv[r, k, d, fields] = jnp.ones((cp, ca), F32)

    def halo_copies(r, k):
        made = []
        n = fields + 1 if (r, k) == (STATOR, 0) else fields
        for d, p, target in ((0, cp - 1, (right, js)), (1, 0, (left, js))):
            made.append(
                pltpu.make_async_remote_copy(
                    src_ref=psend.at[d]
                    if (r, k) == (STATOR, 1)
                    else psi[r][k].at[:, pl.ds(p * cs, cs), :],
                    dst_ref=precv.at[r, k, d, pl.ds(0, n)],
                    send_sem=hs_sem.at[r, k, d],
                    recv_sem=hr_sem.at[r, k, d],
                    device_id=target,
                    device_id_type=MESH,
                )
            )
        for d, target in (
            (0, (ip, lax.rem(js + 1, nspan))),
            (1, (ip, lax.rem(js + nspan - 1, nspan))),
        ):
            made.append(
                pltpu.make_async_remote_copy(
                    src_ref=ssend.at[r, k, d, pl.ds(0, n)],
                    dst_ref=srecv.at[r, k, d, pl.ds(0, n)],
                    send_sem=hs_sem.at[r, k, 2 + d],
                    recv_sem=hr_sem.at[r, k, 2 + d],
                    device_id=target,
                    device_id_type=MESH,
                )
            )
        return made

    halos = {(r, k): halo_copies(r, k) for r in range(2) for k in range(ITERS)}

    def edge(s):
        return pl.ds(s, cp, stride=cs)

    def pack_span(r, k):
        for d, s in ((0, cs - 1), (1, 0)):
            for f in range(psi[r][k].shape[0]):
                ssend[r, k, d, f] = psi[r][k][f, edge(s), :]

    def start_pitch(r, k):
        to_right, to_left = halos[r, k][:2]

        @pl.when(ip == 0)
        def _():
            to_left.start()
            to_right.start()

        @pl.when(ip > 0)
        def _():
            to_right.start()
            to_left.start()

    def start_far(r, k):
        to_right, to_left = halos[r, k][:2]

        @pl.when(ip == 0)
        def _():
            to_left.start()

        @pl.when(ip > 0)
        def _():
            to_right.start()

    def start_near(r, k):
        to_right, to_left = halos[r, k][:2]

        @pl.when(ip == 0)
        def _():
            to_right.start()

        @pl.when(ip > 0)
        def _():
            to_left.start()

    def start_span(r, k):
        to_next, to_prev = halos[r, k][2:]

        @pl.when(has_next)
        def _():
            to_next.start()

        @pl.when(has_prev)
        def _():
            to_prev.start()

    def finish_sends(r, k):
        to_right, to_left, to_next, to_prev = halos[r, k]
        to_right.wait_send()
        to_left.wait_send()

        @pl.when(has_next)
        def _():
            to_next.wait_send()

        @pl.when(has_prev)
        def _():
            to_prev.wait_send()

    def mix(block, f, parts):
        acc = block(f, 0) * parts[0]
        for g in range(1, fields):
            acc = acc + block(f, g) * parts[g]
        return acc

    def span_terms(r, k):
        new = psi[r][k + 1]
        to_next, to_prev = halos[r, k][2:]

        @pl.when(has_prev)
        def _():
            to_next.wait_recv()

        @pl.when(has_next)
        def _():
            to_prev.wait_recv()

        for d, s in ((0, 0), (1, cs - 1)):
            c = coef[r][edge(s), :]
            parts = [srecv[r, k, d, g] for g in range(fields)]
            if (r, k) == (STATOR, 1):
                parts = [x + scor[d, g] for g, x in enumerate(parts)]
            for f in range(fields):
                acc = mix(lambda a, b: blocks[r][a, 3 + d, b], f, parts)
                new[f, edge(s), :] = new[f, edge(s), :] + c * acc

    def add_halos(r, k, send):
        span_terms(r, k)
        inner = face_sums(k + 1, range(1, cp - 1)) if send and r == ROTOR else None
        new = psi[r][k + 1]
        for d, p in ((0, 0), (1, cp - 1)):
            rows = pl.ds(p * cs, cs)
            c = coef[r][rows, :]
            halos[r, k][d].wait_recv()
            parts = [precv[r, k, d, g] for g in range(fields)]
            if (r, k) == (STATOR, 1):
                parts = [x + pcor[d, g] for g, x in enumerate(parts)]
            for f in range(fields):
                acc = mix(lambda a, b: blocks[r][a, 1 + d, b], f, parts)
                value = new[f, rows, :] + c * acc
                new[f, rows, :] = value
                if send and (r, k) == (STATOR, 0):
                    psend[1 - d, f] = value
            if send:
                halos[r, k + 1][1 - d].start()
        if send:
            pack_span(r, k + 1)
            start_span(r, k + 1)
        if inner is not None:
            pack_face(k + 1, inner)
            start_face(k + 1)

    lane = lax.broadcasted_iota(jnp.int32, (cs, ca), 1)
    at_slot = lane - SLOT * lax.broadcasted_iota(jnp.int32, (cs, ca), 0)
    wide = lax.broadcasted_iota(jnp.int32, (nb, ca), 1)

    def face_copy(k, o):
        return pltpu.make_async_remote_copy(
            src_ref=fsend.at[k],
            dst_ref=frecv[k].at[o],
            send_sem=fs_sem.at[k],
            recv_sem=fr_sem.at[k],
            device_id=peer(o),
            device_id_type=MESH,
        )

    def pick(x):
        return jnp.sum(x, axis=1, keepdims=True)

    def face_sums(k, where):
        weights = [jnp.where(p < counts[0], 1.0, 0.0).astype(F32) for p in where]
        sums = []
        for f in range(fields):
            parts = [
                w * psi[ROTOR][k][f, pl.ds(p * cs, cs), :] for w, p in zip(weights, where)
            ]
            while len(parts) > 1:
                parts = [sum(parts[n + 1 : n + 2], parts[n]) for n in range(0, len(parts), 2)]
            sums.append(parts[0])
        return sums

    def pack_face(k, inner):
        count = counts[0]
        ends = face_sums(k, (0, cp - 1))
        sums = [jnp.where(lane == ca - 1, a + b, 0.0) for a, b in zip(inner, ends)]
        tile = jnp.where(at_slot == fields, jnp.clip(count, 0, cp).astype(F32), 0.0)
        for f in range(fields):
            mixed = mix(lambda a, b: iface[a, b], f, sums)
            tile = jnp.where(at_slot == f, pick(mixed), tile)
        row = jnp.sum(tile, axis=0, keepdims=True)
        fsend[k] = row
        frecv[k][0] = row

    def start_face(k):
        each_peer(lambda o: face_copy(k, o).start())

    def all_faces(k):
        return pltpu.make_async_copy(
            frecv[k].at[pl.ds(1, others)], frecv[k].at[pl.ds(1, others)], fr_sem.at[k]
        )

    def sent_faces(k):
        return pltpu.make_async_copy(
            frecv[k].at[pl.ds(1, others)], frecv[k].at[pl.ds(1, others)], fs_sem.at[k]
        )

    def inlets(k, at):
        away = lax.rem(js - source[at] + nspan, nspan)
        total = frecv[k][away]
        for o in range(1, npass):
            total = total + frecv[k][o * nspan + away]
        total = jnp.broadcast_to(total, (cs, ca))
        count = pick(jnp.where(at_slot == fields, total, 0.0))
        made = []
        for f in range(fields):
            value = pick(jnp.where(at_slot == f, total, 0.0)) / count
            made.append(jnp.where(lane == 0, value, 0.0))
        return made

    def add_inlet(k, send):
        all_faces(k).wait()
        new = psi[STATOR][k + 1]
        values = inlets(k, js)

        def add(p):
            rows = pl.ds(p * cs, cs)
            for f in range(fields):
                new[f, rows, :] = new[f, rows, :] + coef[STATOR][rows, :] * values[f]

        add(0)
        add(cp - 1)
        if send:
            start_pitch(STATOR, k + 1)
        for p in range(1, cp - 1):
            add(p)
        if send:
            pack_span(STATOR, k + 1)
            start_span(STATOR, k + 1)
        return values

    def neighbour_inlets(own):
        for d in range(2):
            c = RELAX / precv[STATOR, 0, d, fields]
            for f in range(fields):
                pcor[d, f] = c * own[f]
        for d, s, at, met in (
            (0, cs - 1, jnp.maximum(js - 1, 0), has_prev),
            (1, 0, jnp.minimum(js + 1, nspan - 1), has_next),
        ):
            c = jnp.where(met, 1.0, 0.0) * (RELAX / srecv[STATOR, 0, d, fields])
            values = inlets(0, at)
            for f in range(fields):
                scor[d, f] = c * jnp.broadcast_to(values[f][s : s + 1], (cp, ca))

    def build_matrix(r):
        kk = 5 * nb + 16
        col = lax.broadcasted_iota(jnp.int32, (cs, kk), 1)
        row = lax.broadcasted_iota(jnp.int32, (cs, kk), 0)
        part = col // nb
        g_in = (col - part * nb) // cs
        s_in = col - part * nb - g_in * cs
        which = jnp.full((cs, kk), -1, jnp.int32)
        same = s_in == row
        which = jnp.where((part == 0) & same, 1, which)
        which = jnp.where((part == 2) & same, 2, which)
        which = jnp.where((part == 3) & same, 5, which)
        which = jnp.where((part == 4) & same, 6, which)
        which = jnp.where((part == 1) & (s_in + 1 == row), 3, which)
        which = jnp.where((part == 1) & (s_in == row + 1), 4, which)
        code = jnp.where(which >= 0, which * 8 + g_in, -1)
        middle = jnp.where((part == 1) & same, g_in, -1)
        near, main = [], []
        masks = [[code == (b * 8 + g) for g in range(fields)] for b in range(1, 7)]
        centre = [middle == g for g in range(fields)]
        for f in range(fields):
            acc = jnp.zeros((cs, kk), F32)
            mid = jnp.zeros((cs, kk), F32)
            for g in range(fields):
                mid = jnp.where(centre[g], -RELAX * blocks[r][f, 0, g], mid)
                for b in range(1, 7):
                    acc = jnp.where(masks[b - 1][g], blocks[r][f, b, g], acc)
            near.append(acc)
            main.append(mid)
        hi, lo = split(jnp.concatenate(near + main, axis=0))
        mat[r][pl.ds(0, 2 * nb), :] = hi
        mat[r][pl.ds(2 * nb, 2 * nb), :] = lo

    def clear(r):
        for n in range(2):
            cen[r][n][pl.ds(0, nb), :] = jnp.zeros((nb, ca), BF16)
            cen[r][n][pl.ds((cp + 1) * nb, nb), :] = jnp.zeros((nb, ca), BF16)
            for p in range(cp):
                ext[r][n][pl.ds(p * kx + 2 * nb, 16), :] = jnp.zeros((16, ca), BF16)

    def cell(ref, p):
        return jnp.concatenate([ref[f, pl.ds(p * cs, cs), :] for f in range(fields)], axis=0)

    def store_split(r, k, p):
        new = cell(psi[r][k], p)
        before = jnp.where(wide == 0, 0.0, pltpu.roll(new, 1, 1))
        after = jnp.where(wide == ca - 1, 0.0, pltpu.roll(new, ca - 1, 1))
        for buf, at, value in (
            (cen, (p + 1) * nb, new),
            (ext, p * kx, before),
            (ext, p * kx + nb, after),
        ):
            hi, lo = split(value)
            buf[r][0][pl.ds(at, nb), :] = hi
            buf[r][1][pl.ds(at, nb), :] = lo

    def columns(r, n, p):
        return jnp.concatenate(
            [cen[r][n][pl.ds(p * nb, 3 * nb), :], ext[r][n][pl.ds(p * kx, kx), :]], axis=0
        )

    def interior(r, k):
        for p in range(cp):
            store_split(r, k, p)
        for q in range(cp // 2):
            cells = (2 * q, 2 * q + 1)
            hi = jnp.concatenate([columns(r, 0, p) for p in cells], axis=1)
            lo = jnp.concatenate([columns(r, 1, p) for p in cells], axis=1)
            first = jnp.dot(mat[r][...], hi, preferred_element_type=F32)
            second = jnp.dot(mat[r][pl.ds(0, 2 * nb), :], lo, preferred_element_type=F32)
            both = first[: 2 * nb] + (first[2 * nb :] + second)
            for n, p in enumerate(cells):
                mine = both[:, n * ca : (n + 1) * ca]
                c = coef[r][pl.ds(p * cs, cs), :]
                c = jnp.concatenate([c] * fields, axis=0)
                new = (cell(psi[r][k], p) + mine[nb:]) + c * (cell(rhs[r], p) + mine[:nb])
                for f in range(fields):
                    psi[r][k + 1][f, pl.ds(p * cs, cs), :] = new[f * cs : (f + 1) * cs]

    loads[0].wait()
    pack_span(ROTOR, 0)
    pl.semaphore_wait(barrier, npass + nspan - 2)
    start_far(ROTOR, 0)
    for o in range(1, npass):
        pl.semaphore_signal(
            gate, inc=1, device_id=(lax.rem(ip + o, npass), js), device_id_type=MESH
        )
    for c in loads[1:3]:
        c.wait()
    start_far(STATOR, 0)
    start_near(ROTOR, 0)
    start_span(ROTOR, 0)
    start_near(STATOR, 0)
    pack_span(STATOR, 0)
    start_span(STATOR, 0)
    for c in loads[3:7]:
        c.wait()
    pack_face(0, face_sums(0, range(1, cp - 1)))

    for r in range(2):
        clear(r)
        build_matrix(r)
    for c in loads[7:]:
        c.wait()
    coef[ROTOR][...] = RELAX / coef[ROTOR][...]
    coef[STATOR][...] = RELAX / psi[STATOR][0][fields]
    interior(ROTOR, 0)
    interior(STATOR, 0)
    pl.semaphore_wait(gate, npass - 1)
    start_face(0)

    add_halos(ROTOR, 0, True)
    add_halos(STATOR, 0, True)
    interior(ROTOR, 1)
    neighbour_inlets(add_inlet(0, False))
    interior(STATOR, 1)

    add_halos(ROTOR, 1, True)
    add_halos(STATOR, 1, False)
    add_inlet(1, True)
    interior(ROTOR, 2)
    interior(STATOR, 2)

    for k in range(ITERS - 1):
        for r in range(2):
            finish_sends(r, k)
        sent_faces(k).wait()
    add_halos(ROTOR, 2, False)
    finish_sends(ROTOR, 2)
    sent_faces(2).wait()
    add_inlet(2, False)
    finish_sends(STATOR, 2)
    add_halos(STATOR, 2, False)


def write_out(*refs):
    srcs, dsts, sem = refs[:2], refs[2:4], refs[4]
    copies = [pltpu.make_async_copy(srcs[n], dsts[n], sem.at[n]) for n in range(2)]
    for c in copies:
        c.start()
    for c in copies:
        c.wait()


def per_device(
    npass,
    nspan,
    psi_rotor,
    psi_stator,
    rhs_rotor,
    rhs_stator,
    kappa_rotor,
    kappa_stator,
    rotor_blocks,
    stator_blocks,
    interface_block,
    pass_counts,
    tile_source,
):
    fields, cp, cs, ca = psi_rotor.shape
    shape = (fields, cp * cs, ca)
    flat = [x.reshape(shape) for x in (psi_rotor, psi_stator, rhs_rotor, rhs_stator)]
    kaps = [x.reshape(cp * cs, ca) for x in (kappa_rotor, kappa_stator)]
    small = [x.transpose(1, 0, 2) for x in (rotor_blocks, stator_blocks)]
    small += [interface_block, tile_source]
    nb = fields * cs
    kx = 2 * nb + 16
    state = pltpu.VMEM(shape, F32)
    scratch = [state] * ITERS
    scratch += [pltpu.VMEM((fields + 1, cp * cs, ca), F32)]
    scratch += [state] * (ITERS - 1)
    scratch += [state] * 2
    scratch += [pltpu.VMEM((cp * cs, ca), F32)] * 2
    scratch += [pltpu.VMEM(((cp + 2) * nb, ca), BF16)] * 4
    scratch += [pltpu.VMEM((cp * kx, ca), BF16)] * 4
    scratch += [pltpu.VMEM((4 * nb, 5 * nb + 16), BF16)] * 2
    scratch += [pltpu.SMEM(x.shape, x.dtype) for x in small]
    scratch += [
        pltpu.VMEM((2, ITERS, 2, fields + 1, cs, ca), F32),
        pltpu.VMEM((2, fields, cs, ca), F32),
        pltpu.VMEM((2, ITERS, 2, fields + 1, cp, ca), F32),
        pltpu.VMEM((2, ITERS, 2, fields + 1, cp, ca), F32),
        pltpu.VMEM((ITERS, 1, ca), F32),
        pltpu.VMEM((2, fields, cs, ca), F32),
        pltpu.VMEM((2, fields, cp, ca), F32),
    ]
    scratch += [pltpu.VMEM((npass * nspan, 1, ca), F32)] * ITERS
    dma = pltpu.SemaphoreType.DMA
    scratch += [
        dma((10,)),
        dma((2, ITERS, 4)),
        dma((2, ITERS, 4)),
        dma((ITERS,)),
        dma((ITERS,)),
        pltpu.SemaphoreType.REGULAR,
    ]
    hbm = pl.BlockSpec(memory_space=pltpu.HBM)
    vmem = pl.BlockSpec(memory_space=pltpu.VMEM)
    done = pl.pallas_call(
        functools.partial(kernel, fields, cp, cs, ca, npass, nspan),
        out_shape=[pltpu.VMEM(shape, F32)] * 2,
        in_specs=[hbm] * 10 + [pl.BlockSpec(memory_space=pltpu.SMEM)],
        out_specs=[vmem] * 2,
        scratch_shapes=scratch,
        compiler_params=pltpu.CompilerParams(
            collective_id=0, has_side_effects=True, vmem_limit_bytes=32 * 1024 * 1024
        ),
    )(*[pltpu.with_memory_space_constraint(x, pltpu.HBM) for x in flat + kaps + small], pass_counts)
    out = pl.pallas_call(
        write_out,
        out_shape=[pltpu.HBM(shape, F32)] * 2,
        in_specs=[vmem] * 2,
        out_specs=[hbm] * 2,
        scratch_shapes=[dma((2,))],
    )(*[pltpu.with_memory_space_constraint(x, pltpu.VMEM) for x in done])
    return tuple(x.reshape(psi_rotor.shape) for x in out)


def solution(mesh):
    return jax.shard_map(
        functools.partial(per_device, mesh.shape["passage"], mesh.shape["span"]),
        mesh=mesh,
        in_specs=(
            P(None, "passage", "span", None),
            P(None, "passage", "span", None),
            P(None, "passage", "span", None),
            P(None, "passage", "span", None),
            P("passage", "span", None),
            P("passage", "span", None),
            P(),
            P(),
            P(),
            P("passage"),
            P(),
        ),
        out_specs=(P(None, "passage", "span", None), P(None, "passage", "span", None)),
        check_vma=False,
    )
```
